32 devices in a mesh: row: 4 (over z), col: 8 (over y, x, core).
Axes of the slice: x: 2, y: 2, z: 4, core: 2. Of those that a mesh axis runs over, the one named last changes fastest.
Arguments:
- gate_pre: bfloat16 [512, 16384], P('row', 'col'), may hold values from -6 to 6
- up_pre: bfloat16 [512, 16384], P('row', 'col'), may hold values from -6 to 6
- down_weight: bfloat16 [8192, 16384], P('row', 'col'), may hold values from -0.09375 to 0.09375
- block_mask: int32 [64, 128], P('row', 'col'), may hold values from 0 to 1, as said below
- cotangent: bfloat16 [512, 8192], P('row', 'col'), may hold values from -6 to 6
Outputs:
- output: bfloat16 [512, 8192], P('row', 'col')
- d_gate: bfloat16 [512, 16384], P('row', 'col')
- d_up: bfloat16 [512, 16384], P('row', 'col')
- d_down: bfloat16 [8192, 16384], P('row', 'col')
The draws below stay inside these ranges and needn't reach their ends.
Inputs may be any that keep to these rules, and one draw needn't show every extreme that they name: `block_mask`: each device's tile of 16 x 16 blocks keeps between 64 and 192 blocks; in every draw some tile keeps exactly 192.
All inputs are finite; a program needn't handle non-finite values.
Results may differ from the reference program's by a relative error of at most 0.015.
Values may be sent and summed in bfloat16 or wider, within the bound.
No kernel may reach another device: no remote copies, remote signals or barrier semaphores. Data moves between devices by JAX's collectives and lax.ppermute only.
A program may use at most 128 MiB of HBM per device.

```python
import jax
import jax.numpy as jnp
from jax import lax

D = 8192
FF = 16384
BLK = 128
TOKENS = 512
MASK_R = 64
MASK_C = 128
TILE_R = 16
TILE_C = 16
CAP = 192
N_ROW = 4
N_COL = 8


def draw_block_mask(key, part):
    grid_rows = MASK_R // TILE_R
    grid_cols = MASK_C // TILE_C
    tiles = grid_rows * grid_cols
    block_count = TILE_R * TILE_C
    key_counts, key_top, key_perm = jax.random.split(jax.random.fold_in(key, 17), 3)
    counts = jax.random.randint(key_counts, (tiles,), block_count // 4, CAP + 1)
    top_tile = jax.random.randint(key_top, (), 0, tiles)
    counts = jnp.where(jnp.arange(tiles) == top_tile, CAP, counts)
    perm_keys = jax.random.split(key_perm, tiles)
    perms = jax.vmap(lambda single: jax.random.permutation(single, block_count))(perm_keys)
    kept = (perms < counts[:, None]).astype(jnp.int32)
    shaped = kept.reshape(grid_rows, grid_cols, TILE_R, TILE_C).transpose(0, 2, 1, 3)
    return shaped.reshape(MASK_R, MASK_C)


def strengthened(array, key, source, target, blocks, factor):
    owner, partner = [(jnp.arange(array.shape[axis_at]) // (array.shape[axis_at] // blocks)).reshape([-1 if axis == axis_at else 1 for axis in range(array.ndim)]) for axis_at in (source, target)]
    chosen = jax.random.permutation(key, blocks)[partner]
    strong = (owner == chosen) | (owner == (partner + blocks // 2) % blocks)
    return jnp.where(strong, factor * array, array)


def block_levels(own_key, extent, cuts, smallest, top_value):
    level = 1.0
    for dim, parts in cuts:
        steps = jax.random.uniform(jax.random.fold_in(jax.random.fold_in(own_key, 6), dim), (parts,), jnp.float32, smallest / len(cuts), top_value / len(cuts))
        level = level * jnp.repeat(jnp.exp(steps), extent[dim] // parts).reshape((-1,) + (1,) * (len(extent) - 1 - dim))
    return level


def noise(stream_key, extent, deviation, reach, pieces=(), dtype=jnp.bfloat16):
    result = jax.random.normal(stream_key, extent, jnp.float32) * deviation
    if len(pieces) > 0:
        result = block_levels(stream_key, extent, pieces, -0.22, 0.18) * result
    return jnp.clip(result, min=-reach, max=reach).astype(dtype)


def bell_draw_with(key, shape, spread, limit, cuts, heavy, dtype=jnp.bfloat16):
    array = spread * jax.random.normal(key, shape, jnp.float32)
    if cuts:
        array = array * block_levels(key, shape, cuts, -0.22, 0.18)
    return jnp.clip(strengthened(array, jax.random.fold_in(key, 3), *heavy), -limit, limit).astype(dtype)


def setup_inputs(seed: int = 0) -> dict:
    streams_of = jax.random.split(jax.random.key(seed), 6)
    gate_pre = noise(streams_of[0], (TOKENS, FF), 1.0, 6.0, ((0, 4), (1, 8)))
    up_pre = noise(streams_of[1], (TOKENS, FF), 1.0, 6.0, ((0, 4), (1, 8)))
    down_weight = bell_draw_with(streams_of[2], (D, FF), (FF // 2) ** -0.5, 0.09375, ((0, 4), (1, 8)), (1, 0, 8, 2.0))
    block_mask = draw_block_mask(jax.random.fold_in(streams_of[5], 71), 0)
    cotangent = noise(streams_of[4], (TOKENS, D), 1.0, 6.0, ((0, 4), (1, 8)))
    return dict(gate_pre=gate_pre, up_pre=up_pre, down_weight=down_weight, block_mask=block_mask, cotangent=cotangent)


def reference(gate_pre, up_pre, down_weight, block_mask, cotangent):
    gate_wide = gate_pre.astype(jnp.float32)
    up_wide = up_pre.astype(jnp.float32)
    activated = jax.nn.silu(gate_wide)
    hidden = (activated * up_wide).astype(jnp.bfloat16)
    expand = jnp.repeat(jnp.repeat(block_mask, BLK, axis=0), BLK, axis=1)
    masked = jnp.where(expand > 0, down_weight, jnp.zeros_like(down_weight))
    group = FF // N_COL
    total = jnp.zeros((TOKENS, D), jnp.float32)
    for column in range(N_COL):
        lhs = hidden[:, column * group:(column + 1) * group]
        rhs = masked[:, column * group:(column + 1) * group]
        part = lax.dot_general(lhs, rhs, (((1,), (1,)), ((), ())), preferred_element_type=jnp.float32)
        part = lax.optimization_barrier(part.astype(jnp.bfloat16))
        total = total + part.astype(jnp.float32)
    output = total.astype(jnp.bfloat16)
    width_group = D // N_ROW
    d_hidden = jnp.zeros((TOKENS, FF), jnp.float32)
    for rowgroup in range(N_ROW):
        lhs = cotangent[:, rowgroup * width_group:(rowgroup + 1) * width_group]
        rhs = masked[rowgroup * width_group:(rowgroup + 1) * width_group, :]
        back = jnp.dot(lhs, rhs, preferred_element_type=jnp.float32)
        back = lax.optimization_barrier(back.astype(jnp.bfloat16))
        d_hidden = d_hidden + back.astype(jnp.float32)
    sigmoid_g = jax.nn.sigmoid(gate_wide)
    d_gate = (d_hidden * up_wide * sigmoid_g * (1.0 + gate_wide * (1.0 - sigmoid_g))).astype(jnp.bfloat16)
    d_up = (d_hidden * activated).astype(jnp.bfloat16)
    grad_full = lax.dot_general(cotangent, hidden, (((0,), (0,)), ((), ())), preferred_element_type=jnp.float32)
    d_down = jnp.where(expand > 0, grad_full, jnp.zeros_like(grad_full)).astype(jnp.bfloat16)
    return output, d_gate, d_up, d_down
```

```python
import jax
import jax.numpy as jnp
from jax import lax
from jax.experimental import pallas as pl
from jax.experimental.pallas import tpu as pltpu
from jax.sharding import PartitionSpec as P

F32 = jnp.float32
BF16 = jnp.bfloat16
VMEM = pl.BlockSpec(memory_space=pltpu.VMEM)
SMEM = pl.BlockSpec(memory_space=pltpu.SMEM)
PARAMS = pltpu.CompilerParams(vmem_limit_bytes=40 * 2**20)


def in_vmem(array):
    return pltpu.with_memory_space_constraint(array, pltpu.VMEM)


def place():
    col = lax.axis_index("col")
    return lax.axis_index("row"), col // 2, col % 2


def call(kernel, name, outs, *args, specs=None, scratch=(), flops=0):
    moved = sum(a.size * a.dtype.itemsize for a in args)
    return pl.pallas_call(
        kernel,
        in_specs=specs or [VMEM] * len(args),
        out_specs=[VMEM] * len(outs),
        out_shape=[pltpu.VMEM(shape, dtype) for shape, dtype in outs],
        scratch_shapes=list(scratch),
        compiler_params=PARAMS,
        cost_estimate=pl.CostEstimate(flops=flops, bytes_accessed=moved, transcendentals=0),
        name=name,
    )(*args)


def masked_weight(weight, mask):
    rows, cols = weight.shape
    tile_r, tile_c = mask.shape
    size_r, size_c = rows // tile_r, cols // tile_c

    def kernel(w_ref, m_ref, o_ref, sem):
        def copy(i):
            part = pl.ds(i * size_r, size_r)
            return pltpu.make_async_copy(w_ref.at[part], o_ref.at[part], sem.at[i])

        for i in range(tile_r):
            copy(i).start()
        for i in range(tile_r):
            copy(i).wait()
            for j in range(tile_c):

                @pl.when(m_ref[i, j] == 0)
                def _():
                    o_ref[i * size_r : (i + 1) * size_r, j * size_c : (j + 1) * size_c] = (
                        jnp.zeros((size_r, size_c), BF16)
                    )

    return call(
        kernel,
        "masked_weight",
        [((rows, cols), BF16)],
        weight,
        mask,
        specs=[pl.BlockSpec(memory_space=pl.ANY), SMEM],
        scratch=[pltpu.SemaphoreType.DMA((tile_r,))],
    )[0]


def quarters(cot, chips):
    tok, width = cot.shape
    part = tok // chips

    def kernel(x_ref, *outs):
        _, a, _ = place()
        for u in range(chips):
            outs[u][...] = x_ref[pl.ds(pl.multiple_of((a ^ u) * part, part), part), :]

    return call(kernel, "quarters", [((part, width), BF16)] * chips, in_vmem(cot))


def choose(pieces, order):
    n = len(pieces)

    def kernel(*refs):
        r, a, _ = place()
        for i, t in enumerate(order):
            for u in range(n):

                @pl.when((r ^ a ^ t) == u)
                def _():
                    refs[n + i][...] = refs[u][...]

    shape = (pieces[0].shape, BF16)
    return call(kernel, "choose", [shape] * len(order), *map(in_vmem, pieces))


def back_product(parts, weight, tok):
    chips = len(parts[0])
    flat = [piece for half in parts for piece in half]
    chunk, width = flat[0].shape
    part = tok // chips
    blocks = chunk // part
    dr, ff = weight.shape
    step = 512

    def kernel(*refs):
        w_ref = refs[len(flat)]
        c_ref, *outs = refs[len(flat) + 1 :]
        _, a, h = place()
        for w in range(2):
            lanes = pl.ds(pl.multiple_of((h ^ w) * width, width), width)
            for u in range(chips):
                for b in range(blocks):
                    rows = pl.ds(pl.multiple_of(b * tok + (a ^ u) * part, part), part)
                    c_ref[rows, lanes] = refs[w * chips + u][b * part : (b + 1) * part, :]
        for j in range(0, ff, step):
            product = jnp.dot(
                c_ref[...], w_ref[:, j : j + step], preferred_element_type=F32
            ).astype(BF16)
            for b in range(blocks):
                outs[b][:, j : j + step] = product[b * tok : (b + 1) * tok]

    return call(
        kernel,
        "back_product",
        [((blocks * tok, dr), BF16)] + [((tok, ff), BF16)] * blocks,
        *map(in_vmem, flat),
        in_vmem(weight),
        flops=2 * blocks * tok * dr * ff,
    )


def out_product(hidden, weight, own, dtype):
    tok, ff = hidden[0].shape
    half = weight.shape[0] // 2
    n = len(hidden)
    step = 512

    def kernel(*refs):
        w_ref, o_ref = refs[n:]
        _, _, h = place()
        first = (h if own else 1 - h) * half
        lhs = jnp.concatenate([ref[...] for ref in refs[:n]], axis=0)
        for j in range(0, half, step):
            rows = pl.ds(pl.multiple_of(first + j, step), step)
            o_ref[:, j : j + step] = lax.dot_general(
                lhs, w_ref[rows, :], (((1,), (1,)), ((), ())), preferred_element_type=F32
            ).astype(dtype)

    return call(
        kernel,
        "out_product",
        [((n * tok, half), dtype)],
        *map(in_vmem, hidden),
        in_vmem(weight),
        flops=2 * n * tok * half * ff,
    )[0]


def pair_sum(own, received, tok, chips):
    rows, width = own.shape
    blocks, part = rows // tok, tok // chips

    def kernel(x_ref, y_ref, *outs):
        _, a, _ = place()
        for u in range(chips):
            for b in range(blocks):
                at = pl.ds(pl.multiple_of(b * tok + (a ^ u) * part, part), part)
                outs[u][b * part : (b + 1) * part, :] = (
                    x_ref[at, :] + y_ref[at, :].astype(F32)
                ).astype(BF16)

    return call(
        kernel,
        "pair_sum",
        [((blocks * part, width), BF16)] * chips,
        in_vmem(own),
        in_vmem(received),
    )


def plane_sum(chunks, orders, part):
    flat = [piece for chunk in chunks for piece in chunk]
    chips = len(chunks[0])
    width = flat[0].shape[1]
    count = sum(map(len, orders))

    def kernel(*refs):
        outs = refs[len(flat) :]
        r, a, _ = place()
        for i, order in enumerate(orders):
            for b, t in enumerate(order):
                total = jnp.zeros((part, width), F32)
                for u in range(chips):
                    total += refs[i * chips + u][b * part : (b + 1) * part, :].astype(F32)
                total = total.astype(BF16)
                for k in range(count):

                    @pl.when((r ^ a ^ k) == t)
                    def _():
                        outs[k][...] = total

    return call(
        kernel, "plane_sum", [((part, width), BF16)] * count, *map(in_vmem, flat)
    )


def assemble(pieces):
    n = len(pieces)
    part, width = pieces[0].shape

    def kernel(*refs):
        r, _, _ = place()
        for k in range(n):
            refs[n][pl.ds(pl.multiple_of((r ^ k) * part, part), part), :] = refs[k][...]

    return pl.pallas_call(
        kernel,
        in_specs=[VMEM] * n,
        out_specs=VMEM,
        out_shape=jax.ShapeDtypeStruct((n * part, width), BF16),
        compiler_params=PARAMS,
        name="assemble",
    )(*map(in_vmem, pieces))


def down_gradient(cots, hidden, mask):
    tok, ff = hidden[0].shape
    dr = cots[0].shape[1]
    tokens = tok * len(hidden)
    tile_r, tile_c = mask.shape
    size_r, size_c = dr // tile_r, ff // tile_c
    step = 512
    nc, nh = len(cots), len(hidden)

    def kernel(*refs):
        m_ref, o_ref, h_all, c_all = refs[nc + nh :]
        i = pl.program_id(0)

        @pl.when(i == 0)
        def _():
            for t in range(nh):
                h_all[t * tok : (t + 1) * tok, :] = refs[nc + t][...]

        at = 0
        for c in range(nc):
            c_all[at : at + cots[c].shape[0], :] = refs[c][...]
            at += cots[c].shape[0]
        o_ref[...] = lax.dot_general(
            c_all[...], h_all[...], (((0,), (0,)), ((), ())), preferred_element_type=F32
        ).astype(BF16)
        for b in range(step // size_r):
            for j in range(tile_c):

                @pl.when(m_ref[i * (step // size_r) + b, j] == 0)
                def _():
                    o_ref[b * size_r : (b + 1) * size_r, j * size_c : (j + 1) * size_c] = (
                        jnp.zeros((size_r, size_c), BF16)
                    )

    return pl.pallas_call(
        kernel,
        grid=(dr // step,),
        in_specs=[pl.BlockSpec((c.shape[0], step), lambda i: (0, i)) for c in cots]
        + [VMEM] * nh
        + [SMEM],
        out_specs=pl.BlockSpec((step, ff), lambda i: (i, 0)),
        out_shape=jax.ShapeDtypeStruct((dr, ff), BF16),
        scratch_shapes=[pltpu.VMEM((tokens, ff), BF16), pltpu.VMEM((tokens, step), BF16)],
        compiler_params=PARAMS,
        cost_estimate=pl.CostEstimate(
            flops=2 * tokens * dr * ff, bytes_accessed=2 * dr * ff, transcendentals=0
        ),
        name="down_gradient",
    )(*map(in_vmem, cots), *map(in_vmem, hidden), mask)


def fast_body(gate_pre, up_pre, down_weight, block_mask, cotangent):
    rows, chips = 4, 4
    tok = gate_pre.shape[0]
    part = tok // chips

    def over_row(x, t):
        return lax.ppermute(x, "row", [(i, i ^ t) for i in range(rows)])

    def over_chips(x, u):
        return lax.ppermute(x, "col", [(j, j ^ (2 * u)) for j in range(2 * chips)])

    def over_core(x):
        return lax.ppermute(x, "col", [(j, j ^ 1) for j in range(2 * chips)])

    spread = quarters(cotangent, chips)
    spread = [spread[0]] + [over_chips(spread[u], u) for u in range(1, chips)]

    gate_wide = gate_pre.astype(F32)
    up_wide = up_pre.astype(F32)
    activated = jax.nn.silu(gate_wide)
    hidden = {0: (activated * up_wide).astype(BF16)}
    hidden[1] = over_row(hidden[0], 1)
    hidden[3] = over_row(hidden[0], 3)

    weight = masked_weight(down_weight, block_mask)

    ours = choose(spread, (2, 3, 1, 0))
    cot = {t: over_row(x, t) for t, x in zip((2, 3, 1), ours)}
    cot[0] = ours[3]

    chunk_cot, back = [], {}
    for order in ((2, 3), (1, 0)):
        mine = jnp.concatenate([cot[t] for t in order], axis=0)
        same = [mine] + [over_chips(mine, u) for u in range(1, chips)]
        other = [over_core(x) for x in same]
        gathered, *blocks = back_product([same, other], weight, tok)
        chunk_cot.append(gathered)
        back.update(zip(order, blocks))

    near = over_row(back[2], 1)
    paired = (back[3].astype(F32) + near.astype(F32)).astype(BF16)
    far = over_row(paired, 3)
    beside = over_row(back[1], 1)
    d_hidden = back[0].astype(F32) + beside.astype(F32) + far.astype(F32)
    sigmoid_g = jax.nn.sigmoid(gate_wide)
    d_gate = (d_hidden * up_wide * sigmoid_g * (1.0 + gate_wide * (1.0 - sigmoid_g))).astype(BF16)
    d_up = (d_hidden * activated).astype(BF16)

    hidden[2] = over_row(hidden[3], 1)

    orders = ((0, 1, 3), (2,))
    sums = []
    for order in orders:
        blocks = [hidden[t] for t in order]
        received = over_core(out_product(blocks, weight, False, BF16))
        pieces = pair_sum(out_product(blocks, weight, True, F32), received, tok, chips)
        sums.append([pieces[0]] + [over_chips(pieces[u], u) for u in range(1, chips)])
    ready = plane_sum(sums, orders, part)
    width = 2 * chips
    placed = [
        lax.ppermute(
            ready[k],
            ("row", "col"),
            [
                (r * width + 2 * a + h, (a ^ k) * width + 2 * r + h)
                for r in range(rows)
                for a in range(chips)
                for h in range(2)
            ],
        )
        for k in range(rows)
    ]
    output = assemble(placed)

    d_down = down_gradient(chunk_cot, [hidden[t] for t in (2, 3, 1, 0)], block_mask)
    return output, d_gate, d_up, d_down


def rounded_f32(values):
    return lax.optimization_barrier(values.astype(BF16)).astype(F32)


def general_body(gate_pre, up_pre, down_weight, block_mask, cotangent):
    tok_rows, ff_cols = gate_pre.shape
    d_rows = down_weight.shape[0]
    block_size = d_rows // block_mask.shape[0]
    gate_wide = gate_pre.astype(F32)
    up_wide = up_pre.astype(F32)
    activated = jax.nn.silu(gate_wide)
    hidden = (activated * up_wide).astype(BF16)
    expand = jnp.repeat(jnp.repeat(block_mask, block_size, axis=0), block_size, axis=1)
    masked = jnp.where(expand > 0, down_weight, jnp.zeros_like(down_weight))
    cot_row = lax.all_gather(cotangent, "col", axis=1, tiled=True)
    cot_all = lax.all_to_all(cot_row, "row", split_axis=1, concat_axis=0, tiled=True)
    panel = lax.all_gather(masked, "row", axis=0, tiled=True)
    y_partial = lax.dot_general(
        hidden, panel, (((1,), (1,)), ((), ())), preferred_element_type=F32
    )
    shards = panel.shape[0] // d_rows
    per_shard = jnp.einsum(
        "tnd,ndf->ntf",
        cot_row.reshape(tok_rows, shards, d_rows),
        panel.reshape(shards, d_rows, ff_cols),
        preferred_element_type=F32,
    )
    d_hidden = jnp.sum(rounded_f32(per_shard), axis=0)
    hidden_all = lax.all_gather(hidden, "row", axis=0, tiled=True)
    grad_full = lax.dot_general(
        cot_all, hidden_all, (((0,), (0,)), ((), ())), preferred_element_type=F32
    )
    output = lax.psum_scatter(y_partial.astype(BF16), "col", scatter_dimension=1, tiled=True)
    sigmoid_g = jax.nn.sigmoid(gate_wide)
    d_gate = (d_hidden * up_wide * sigmoid_g * (1.0 + gate_wide * (1.0 - sigmoid_g))).astype(BF16)
    d_up = (d_hidden * activated).astype(BF16)
    d_down = jnp.where(expand > 0, grad_full, jnp.zeros_like(grad_full)).astype(BF16)
    return output, d_gate, d_up, d_down


def solution(mesh):
    spec = P("row", "col")
    small = mesh.shape["row"] == 4 and mesh.shape["col"] == 8
    return jax.shard_map(
        fast_body if small else general_body,
        mesh=mesh,
        in_specs=(spec,) * 5,
        out_specs=(spec,) * 4,
        check_vma=False,
    )
```

```python
import jax
import jax.numpy as jnp
from jax import lax
from jax.experimental import pallas as pl
from jax.experimental.pallas import tpu as pltpu
from jax.sharding import PartitionSpec as P

F32 = jnp.float32
BF16 = jnp.bfloat16
VMEM = pl.BlockSpec(memory_space=pltpu.VMEM)
SMEM = pl.BlockSpec(memory_space=pltpu.SMEM)
PARAMS = pltpu.CompilerParams(vmem_limit_bytes=16 * 2**20)


ANY = pl.BlockSpec(memory_space=pl.ANY)


def in_vmem(array):
    return pltpu.with_memory_space_constraint(array, pltpu.VMEM)


def in_hbm(array):
    return pltpu.with_memory_space_constraint(array, pltpu.HBM)


def place():
    col = lax.axis_index("col")
    return lax.axis_index("row"), col // 2, col % 2


def call(kernel, name, outs, *args, specs=None, scratch=(), flops=0, moved=0, after=()):
    n, m = len(args), len(args) + len(after)

    def body(*refs):
        kernel(*refs[:n], *refs[m:])

    return pl.pallas_call(
        body,
        in_specs=(specs or [VMEM] * n) + [pl.BlockSpec(memory_space=pl.ANY)] * len(after),
        out_specs=[VMEM] * len(outs),
        out_shape=[pltpu.VMEM(shape, dtype) for shape, dtype in outs],
        scratch_shapes=list(scratch),
        compiler_params=PARAMS,
        cost_estimate=pl.CostEstimate(flops=flops, bytes_accessed=moved, transcendentals=0),
        name=name,
    )(*args, *after)


def masked_weight(weight, mask, after=()):
    rows, cols = weight.shape
    tile_r, tile_c = mask.shape
    size_r, size_c = rows // tile_r, cols // tile_c

    def kernel(w_ref, m_ref, o_ref, sem):
        def copy(i):
            part = pl.ds(i * size_r, size_r)
            return pltpu.make_async_copy(w_ref.at[part], o_ref.at[part], sem.at[i])

        for i in range(tile_r):
            copy(i).start()
        for i in range(tile_r):
            copy(i).wait()
            for j in range(tile_c):

                @pl.when(m_ref[i, j] == 0)
                def _():
                    o_ref[i * size_r : (i + 1) * size_r, j * size_c : (j + 1) * size_c] = (
                        jnp.zeros((size_r, size_c), BF16)
                    )

    return call(
        kernel,
        "masked_weight",
        [((rows, cols), BF16)],
        in_hbm(weight),
        mask,
        specs=[ANY, SMEM],
        scratch=[pltpu.SemaphoreType.DMA((tile_r,))],
        after=after,
    )[0]


def gated(gate, up, after=()):
    def kernel(g_hbm, u_hbm, o_ref, dg_ref, du_ref, g_ref, u_ref, sem):
        copies = [
            pltpu.make_async_copy(g_hbm, g_ref, sem.at[0]),
            pltpu.make_async_copy(u_hbm, u_ref, sem.at[1]),
        ]
        for copy in copies:
            copy.start()
        for copy in copies:
            copy.wait()
        g = g_ref[...].astype(F32)
        u = u_ref[...].astype(F32)
        s = 1.0 / (1.0 + jnp.exp(-g))
        o_ref[...] = (g * s * u).astype(BF16)
        dg_ref[...] = u * s * (1.0 + g * (1.0 - s))
        du_ref[...] = g * s

    return call(
        kernel,
        "gated",
        [(gate.shape, BF16), (gate.shape, F32), (gate.shape, F32)],
        in_hbm(gate),
        in_hbm(up),
        specs=[ANY] * 2,
        scratch=[pltpu.VMEM(gate.shape, BF16)] * 2 + [pltpu.SemaphoreType.DMA((2,))],
        after=after,
    )


def gradients(shares, dg, du, after=()):
    rows, cols = dg.shape
    n = len(shares)
    step = rows // 4

    def kernel(*refs):
        dg_ref, du_ref = refs[n : n + 2]
        out_g, out_u = refs[-2:]
        total = refs[0][...].astype(F32)
        for ref in refs[1:n]:
            total += ref[...].astype(F32)
        out_g[...] = (total * dg_ref[...]).astype(BF16)
        out_u[...] = (total * du_ref[...]).astype(BF16)

    block = pl.BlockSpec((step, cols), lambda i: (i, 0))
    return pl.pallas_call(
        kernel,
        grid=(rows // step,),
        in_specs=[block] * (n + 2) + [ANY] * len(after),
        out_specs=[block] * 2,
        out_shape=[jax.ShapeDtypeStruct((rows, cols), BF16)] * 2,
        compiler_params=PARAMS,
        name="gradients",
    )(*map(in_vmem, shares), in_vmem(dg), in_vmem(du), *after)


def stack(pieces, after=()):
    part, width = pieces[0].shape

    def kernel(*refs):
        for i in range(len(pieces)):
            refs[-1][i * part : (i + 1) * part, :] = refs[i][...]

    shape = (len(pieces) * part, width)
    return call(kernel, "stack", [(shape, BF16)], *map(in_vmem, pieces), after=after)[0]


def quarters(cot, chips):
    tok, width = cot.shape
    part = tok // chips

    def kernel(x_ref, *rest):
        outs, sem = rest[:chips], rest[chips]
        _, a, _ = place()
        copies = [
            pltpu.make_async_copy(
                x_ref.at[pl.ds(pl.multiple_of((a ^ u) * part, part), part)], outs[u], sem.at[u]
            )
            for u in range(chips)
        ]
        for copy in copies:
            copy.start()
        for copy in copies:
            copy.wait()

    return call(
        kernel,
        "quarters",
        [((part, width), BF16)] * chips,
        in_hbm(cot),
        specs=[ANY],
        scratch=[pltpu.SemaphoreType.DMA((chips,))],
    )


def choose(pieces, order, after=()):
    n = len(pieces)

    def kernel(*refs):
        r, a, _ = place()
        for i, t in enumerate(order):
            for u in range(n):

                @pl.when((r ^ a ^ t) == u)
                def _():
                    refs[n + i][...] = refs[u][...]

    shape = (pieces[0].shape, BF16)
    return call(kernel, "choose", [shape] * len(order), *map(in_vmem, pieces), after=after)


def back_product(own, other, weight, tok, after=()):
    chips = len(own)
    chunk, width = own[0].shape
    part = tok // chips
    blocks = chunk // part
    dr, ff = weight.shape
    step = 512

    def kernel(*refs):
        x_ref, w_ref, c_ref, out2, out3 = refs[chips:]
        _, a, h = place()
        for w in range(2):
            lanes = pl.ds(pl.multiple_of((h ^ w) * width, width), width)
            for u in range(chips):
                for t in range(blocks):
                    rows = pl.ds(pl.multiple_of(t * tok + (a ^ u) * part, part), part)
                    if w == 0:
                        c_ref[rows, lanes] = refs[u][t * part : (t + 1) * part, :]
                    else:
                        at = u * chunk + t * part
                        c_ref[rows, lanes] = x_ref[at : at + part, :]
        for j in range(0, ff, step):
            product = jnp.dot(
                c_ref[2 * tok : 4 * tok, :], w_ref[:, j : j + step], preferred_element_type=F32
            ).astype(BF16)
            out2[:, j : j + step] = product[:tok]
            out3[:, j : j + step] = product[tok:]

    return call(
        kernel,
        "back_product",
        [((blocks * tok, dr), BF16)] + [((tok, ff), BF16)] * 2,
        *map(in_vmem, own),
        in_vmem(other),
        in_vmem(weight),
        flops=4 * tok * dr * ff,
        after=after,
    )


def back_rest(cot, weight, tok, passed, after=()):
    dr, ff = weight.shape
    step = 512

    def kernel(c_ref, w_ref, p_ref, out0, out1, out_p):
        out_p[...] = p_ref[...]
        for j in range(0, ff, step):
            product = jnp.dot(
                c_ref[: 2 * tok, :], w_ref[:, j : j + step], preferred_element_type=F32
            ).astype(BF16)
            out0[:, j : j + step] = product[:tok]
            out1[:, j : j + step] = product[tok:]

    return call(
        kernel,
        "back_rest",
        [((tok, ff), BF16)] * 3,
        in_vmem(cot),
        in_vmem(weight),
        in_vmem(passed),
        flops=4 * tok * dr * ff,
        after=after,
    )


def out_product(hidden, pair, weight, after=()):
    tok, ff = pair[0].shape
    half = weight.shape[0] // 2
    n = len(hidden)
    step = 512

    def kernel(*refs):
        x_ref, y_ref, w_ref, *sent, own_ref, block_ref = refs[n:]
        _, _, h = place()
        block_ref[...] = x_ref[...] + y_ref[...]
        lhs = jnp.concatenate([ref[...] for ref in refs[:n]] + [block_ref[...]], axis=0)
        for j in range(0, half, step):
            for own, first in ((False, (1 - h) * half), (True, h * half)):
                at = pl.ds(pl.multiple_of(first + j, step), step)
                product = lax.dot_general(
                    lhs, w_ref[at, :], (((1,), (1,)), ((), ())), preferred_element_type=F32
                )
                if own:
                    own_ref[:, j : j + step] = product
                else:
                    sent[j // step][...] = product.astype(BF16)

    rows = (n + 1) * tok
    return call(
        kernel,
        "out_product",
        [((rows, step), BF16)] * (half // step) + [((rows, half), F32), ((tok, ff), BF16)],
        *map(in_vmem, hidden),
        *map(in_vmem, pair),
        in_vmem(weight),
        flops=4 * max(rows, 256) * half * ff,
        after=after,
    )


def add_and_pass(pairs, passed=(), after=()):
    flat = [x for pair in pairs for x in pair]

    def kernel(*refs):
        outs = refs[len(flat) + len(passed) :]
        for i in range(len(pairs)):
            outs[i][...] = (
                refs[2 * i][...].astype(F32) + refs[2 * i + 1][...].astype(F32)
            ).astype(BF16)
        for i in range(len(passed)):
            outs[len(pairs) + i][...] = refs[len(flat) + i][...]

    shapes = [(pair[0].shape, BF16) for pair in pairs] + [(x.shape, BF16) for x in passed]
    return call(
        kernel, "add_and_pass", shapes, *map(in_vmem, flat), *map(in_vmem, passed), after=after
    )


def pair_sum(own, received, tok, chips, after=()):
    rows, width = own.shape
    blocks, part = rows // tok, tok // chips

    step = received[0].shape[1]

    def kernel(x_ref, *refs):
        outs = refs[len(received) :]
        _, a, _ = place()
        for u in range(chips):
            for b in range(blocks):
                at = pl.ds(pl.multiple_of(b * tok + (a ^ u) * part, part), part)
                for i in range(len(received)):
                    lanes = slice(i * step, (i + 1) * step)
                    outs[u][b * part : (b + 1) * part, lanes] = (
                        x_ref[at, lanes] + refs[i][at, :].astype(F32)
                    ).astype(BF16)

    return call(
        kernel,
        "pair_sum",
        [((blocks * part, width), BF16)] * chips,
        in_vmem(own),
        *map(in_vmem, received),
        after=after,
    )


def early_sum(pieces, after=()):
    def kernel(*refs):
        total = refs[0][...].astype(F32)
        for ref in refs[1:-1]:
            total += ref[...].astype(F32)
        refs[-1][...] = total.astype(BF16)

    shape = (pieces[0].shape, BF16)
    return call(kernel, "early_sum", [shape], *map(in_vmem, pieces), after=after)[0]


def plane_sum(early, pieces, part, after=()):
    n = len(pieces)
    blocks = early.shape[0] // part + 1

    def kernel(*refs):
        outs = refs[n + 1 :]
        r, a, _ = place()
        total = refs[1][...].astype(F32)
        for ref in refs[2 : n + 1]:
            total += ref[...].astype(F32)
        sums = [refs[0][t * part : (t + 1) * part, :] for t in range(blocks - 1)]
        for t, value in enumerate(sums + [total.astype(BF16)]):
            for k in range(blocks):

                @pl.when((r ^ a ^ k) == t)
                def _():
                    outs[k][...] = value

    return call(
        kernel,
        "plane_sum",
        [(pieces[0].shape, BF16)] * blocks,
        in_vmem(early),
        *map(in_vmem, pieces),
        after=after,
    )


def assemble(pieces):
    n = len(pieces)
    part, width = pieces[0].shape

    def kernel(*refs):
        r, _, _ = place()
        for k in range(n):
            refs[n][pl.ds(pl.multiple_of((r ^ k) * part, part), part), :] = refs[k][...]

    return pl.pallas_call(
        kernel,
        in_specs=[VMEM] * n,
        out_specs=VMEM,
        out_shape=jax.ShapeDtypeStruct((n * part, width), BF16),
        compiler_params=PARAMS,
        name="assemble",
    )(*map(in_vmem, pieces))


def down_gradient(cots, hidden, mask, steps, begun=None, after=()):
    tok, ff = hidden[0].shape
    dr = cots[0].shape[1]
    tokens = tok * len(hidden)
    tile_r, tile_c = mask.shape
    size_r, size_c = dr // tile_r, ff // tile_c
    step = dr // 4
    first, count = steps
    nc, nh = len(cots), len(hidden)
    extra = ([] if begun is None else [begun]) + list(after)

    def kernel(*refs):
        m_ref = refs[nc + nh]
        o_ref, t_ref, h_all, c_all = refs[nc + nh + 1 + len(extra) :]
        t_ref[...] = jnp.zeros(t_ref.shape, BF16)
        i = pl.program_id(0)

        @pl.when(i == 0)
        def _():
            for t in range(nh):
                h_all[t * tok : (t + 1) * tok, :] = refs[nc + t][...]

        at = 0
        for c in range(nc):
            c_all[at : at + cots[c].shape[0], :] = refs[c][...]
            at += cots[c].shape[0]
        o_ref[...] = lax.dot_general(
            c_all[...], h_all[...], (((0,), (0,)), ((), ())), preferred_element_type=F32
        ).astype(BF16)
        for b in range(step // size_r):
            for j in range(tile_c):

                @pl.when(m_ref[(first + i) * (step // size_r) + b, j] == 0)
                def _():
                    o_ref[b * size_r : (b + 1) * size_r, j * size_c : (j + 1) * size_c] = (
                        jnp.zeros((size_r, size_c), BF16)
                    )

    return pl.pallas_call(
        kernel,
        grid=(count,),
        in_specs=[pl.BlockSpec((c.shape[0], step), lambda i: (0, first + i)) for c in cots]
        + [VMEM] * nh
        + [SMEM]
        + [pl.BlockSpec(memory_space=pl.ANY)] * len(extra),
        out_specs=[pl.BlockSpec((step, ff), lambda i: (first + i, 0)), VMEM],
        out_shape=[jax.ShapeDtypeStruct((dr, ff), BF16), pltpu.VMEM((16, 128), BF16)],
        scratch_shapes=[pltpu.VMEM((tokens, ff), BF16), pltpu.VMEM((tokens, step), BF16)],
        input_output_aliases={} if begun is None else {nc + nh + 1: 0},
        compiler_params=PARAMS,
        cost_estimate=pl.CostEstimate(
            flops=2 * tokens * step * count * ff,
            bytes_accessed=2 * step * count * ff,
            transcendentals=0,
        ),
        name="down_gradient",
    )(*map(in_vmem, cots), *map(in_vmem, hidden), mask, *extra)


def fast_body(gate_pre, up_pre, down_weight, block_mask, cotangent):
    rows, chips = 4, 4
    tok = gate_pre.shape[0]
    part = tok // chips

    def over_row(x, t, senders=range(4)):
        return lax.ppermute(x, "row", [(i, i ^ t) for i in senders])

    def over_chips(x, u):
        return lax.ppermute(x, "col", [(j, j ^ (2 * u)) for j in range(2 * chips)])

    def over_core(x):
        return lax.ppermute(x, "col", [(j, j ^ 1) for j in range(2 * chips)])

    ends, inner = (0, 3), (1, 2)

    mine = quarters(cotangent, chips)
    spread = [mine[0]] + [over_chips(mine[u], u) for u in range(1, chips)]
    first, dg, du = gated(gate_pre, up_pre, after=[mine[0]])
    ours = choose(spread, (3, 2, 1, 0), after=[first])
    cot = {t: over_row(x, t) for t, x in zip((3, 2, 1), ours)}
    cot[0] = ours[3]

    weight = masked_weight(down_weight, block_mask, after=[ours[0]])
    hidden = {0: add_and_pass([], [first], after=[weight, cot[1], cot[2], cot[3]])[0]}
    hidden[1] = over_row(hidden[0], 1)
    inner3 = over_row(hidden[0], 3, inner)
    inner2 = over_row(hidden[1], 3, inner)
    ends2 = over_row(inner3, 1, inner)


    mine = stack([cot[t] for t in range(rows)], after=[hidden[0]])
    same = [mine] + [over_chips(mine, u) for u in range(1, chips)]
    other = over_core(stack(same, after=[hidden[1], inner3]))
    cot, back2, back3 = back_product(same, other, weight, tok)

    first3 = over_row(back3, 1, ends)
    first2 = over_row(back2, 1, ends)
    back0, back1, inner2 = back_rest(cot, weight, tok, inner2, after=[back3])
    ends3 = over_row(inner2, 1, inner)

    def to_plane(own, received, after=()):
        pieces = pair_sum(own, received, tok, chips, after=after)
        return [pieces[0]] + [over_chips(pieces[u], u) for u in range(1, chips)]

    *sent, own, hidden[2] = out_product(
        [hidden[0], hidden[1]], [inner2, ends2], weight, after=[back1]
    )
    received = [over_core(x) for x in sent]
    (to_pass,) = add_and_pass([(back2, first3)], after=[own])
    second = over_row(to_pass, 3, inner)
    early = to_plane(own, received, after=[to_pass])

    *sent, own, hidden[3] = out_product([], [inner3, ends3], weight, after=[early[0]])
    received = [over_core(x) for x in sent]
    to_inner, to_near = add_and_pass([(back3, first2), (back1, second)], after=[own])
    across = over_row(to_inner, 3, inner)
    beside = over_row(to_near, 1)
    early = early_sum(early, after=[to_inner])
    late = to_plane(own, received, after=[early])

    tokens = [hidden[t] for t in range(rows)]
    d_down, done = down_gradient([cot], tokens, block_mask, (0, 2), after=[late[0]])
    ready = plane_sum(early, late, part, after=[done])
    d_down, done = down_gradient([cot], tokens, block_mask, (2, 2), d_down, after=[ready[0]])

    d_gate, d_up = gradients([back0, beside, across], dg, du, after=[done])

    width = 2 * chips
    placed = [
        lax.ppermute(
            ready[k],
            ("row", "col"),
            [
                (r * width + 2 * a + h, (a ^ k) * width + 2 * r + h)
                for r in range(rows)
                for a in range(chips)
                for h in range(2)
            ],
        )
        for k in range(rows)
    ]
    output = assemble(placed)

    return output, d_gate, d_up, d_down


def rounded_f32(values):
    return lax.optimization_barrier(values.astype(BF16)).astype(F32)


def general_body(gate_pre, up_pre, down_weight, block_mask, cotangent):
    tok_rows, ff_cols = gate_pre.shape
    d_rows = down_weight.shape[0]
    block_size = d_rows // block_mask.shape[0]
    gate_wide = gate_pre.astype(F32)
    up_wide = up_pre.astype(F32)
    activated = jax.nn.silu(gate_wide)
    hidden = (activated * up_wide).astype(BF16)
    expand = jnp.repeat(jnp.repeat(block_mask, block_size, axis=0), block_size, axis=1)
    masked = jnp.where(expand > 0, down_weight, jnp.zeros_like(down_weight))
    cot_row = lax.all_gather(cotangent, "col", axis=1, tiled=True)
    cot_all = lax.all_to_all(cot_row, "row", split_axis=1, concat_axis=0, tiled=True)
    panel = lax.all_gather(masked, "row", axis=0, tiled=True)
    y_partial = lax.dot_general(
        hidden, panel, (((1,), (1,)), ((), ())), preferred_element_type=F32
    )
    shards = panel.shape[0] // d_rows
    per_shard = jnp.einsum(
        "tnd,ndf->ntf",
        cot_row.reshape(tok_rows, shards, d_rows),
        panel.reshape(shards, d_rows, ff_cols),
        preferred_element_type=F32,
    )
    d_hidden = jnp.sum(rounded_f32(per_shard), axis=0)
    hidden_all = lax.all_gather(hidden, "row", axis=0, tiled=True)
    grad_full = lax.dot_general(
        cot_all, hidden_all, (((0,), (0,)), ((), ())), preferred_element_type=F32
    )
    output = lax.psum_scatter(y_partial.astype(BF16), "col", scatter_dimension=1, tiled=True)
    sigmoid_g = jax.nn.sigmoid(gate_wide)
    d_gate = (d_hidden * up_wide * sigmoid_g * (1.0 + gate_wide * (1.0 - sigmoid_g))).astype(BF16)
    d_up = (d_hidden * activated).astype(BF16)
    d_down = jnp.where(expand > 0, grad_full, jnp.zeros_like(grad_full)).astype(BF16)
    return output, d_gate, d_up, d_down


def solution(mesh):
    spec = P("row", "col")
    small = mesh.shape["row"] == 4 and mesh.shape["col"] == 8
    return jax.shard_map(
        fast_body if small else general_body,
        mesh=mesh,
        in_specs=(spec,) * 5,
        out_specs=(spec,) * 4,
        check_vma=False,
    )
```

```python
import jax
import jax.numpy as jnp
from jax import lax
from jax.experimental import pallas as pl
from jax.experimental.pallas import tpu as pltpu
from jax.sharding import PartitionSpec as P

F32 = jnp.float32
BF16 = jnp.bfloat16
VMEM = pl.BlockSpec(memory_space=pltpu.VMEM)
SMEM = pl.BlockSpec(memory_space=pltpu.SMEM)
PARAMS = pltpu.CompilerParams(vmem_limit_bytes=16 * 2**20)


ANY = pl.BlockSpec(memory_space=pl.ANY)


def in_vmem(array):
    return pltpu.with_memory_space_constraint(array, pltpu.VMEM)


def in_hbm(array):
    return pltpu.with_memory_space_constraint(array, pltpu.HBM)


def place():
    col = lax.axis_index("col")
    return lax.axis_index("row"), col // 2, col % 2


def call(kernel, name, outs, *args, specs=None, scratch=(), flops=0, moved=0, after=()):
    n, m = len(args), len(args) + len(after)

    def body(*refs):
        kernel(*refs[:n], *refs[m:])

    return pl.pallas_call(
        body,
        in_specs=(specs or [VMEM] * n) + [pl.BlockSpec(memory_space=pl.ANY)] * len(after),
        out_specs=[VMEM] * len(outs),
        out_shape=[pltpu.VMEM(shape, dtype) for shape, dtype in outs],
        scratch_shapes=list(scratch),
        compiler_params=PARAMS,
        cost_estimate=pl.CostEstimate(flops=flops, bytes_accessed=moved, transcendentals=0),
        name=name,
    )(*args, *after)


def masked_weight(weight, mask_rows, half, begun=None, after=()):
    rows, cols = weight.shape
    tile_r = mask_rows.shape[0]
    size = rows // tile_r
    mine = range(half * tile_r // 2, (half + 1) * tile_r // 2)
    extra = [] if begun is None else [in_vmem(begun)]

    def kernel(w_ref, m_ref, *refs):
        o_ref, sem = refs[-2:]

        def copy(i):
            at = pl.ds(i * size, size)
            return pltpu.make_async_copy(w_ref.at[at], o_ref.at[at], sem.at[i - mine[0]])

        for i in mine:
            copy(i).start()
        for i in mine:
            copy(i).wait()
            at = slice(i * size, (i + 1) * size)
            o_ref[at, :] = jnp.where(m_ref[i : i + 1, :] > 0, o_ref[at, :], jnp.zeros((), BF16))

    return pl.pallas_call(
        kernel,
        in_specs=[ANY, VMEM] + [VMEM] * len(extra) + [ANY] * len(after),
        out_specs=VMEM,
        out_shape=pltpu.VMEM((rows, cols), BF16),
        input_output_aliases={} if begun is None else {2: 0},
        scratch_shapes=[pltpu.SemaphoreType.DMA((len(mine),))],
        compiler_params=PARAMS,
        cost_estimate=pl.CostEstimate(flops=0, bytes_accessed=0, transcendentals=0),
        name="masked_weight",
    )(in_hbm(weight), in_vmem(mask_rows), *extra, *after)


def gated(gate, up, mask, width, after=()):
    tile_r, tile_c = mask.shape
    size = width // tile_c

    def kernel(g_hbm, u_hbm, m_hbm, o_ref, dg_ref, du_ref, rows_ref, g_ref, u_ref, m_ref, sem):
        copies = [
            pltpu.make_async_copy(m_hbm, m_ref, sem.at[2]),
            pltpu.make_async_copy(g_hbm, g_ref, sem.at[0]),
            pltpu.make_async_copy(u_hbm, u_ref, sem.at[1]),
        ]
        for copy in copies:
            copy.start()
        copies[0].wait()
        for i in range(tile_r):
            for j in range(tile_c):
                rows_ref[i : i + 1, j * size : (j + 1) * size] = jnp.full(
                    (1, size), m_ref[i, j], jnp.int32
                )
        for copy in copies[1:]:
            copy.wait()
        g = g_ref[...].astype(F32)
        u = u_ref[...].astype(F32)
        s = 1.0 / (1.0 + jnp.exp(-g))
        o_ref[...] = (g * s * u).astype(BF16)
        dg_ref[...] = u * s * (1.0 + g * (1.0 - s))
        du_ref[...] = g * s

    return call(
        kernel,
        "gated",
        [
            (gate.shape, BF16),
            (gate.shape, F32),
            (gate.shape, F32),
            ((tile_r, width), jnp.int32),
        ],
        in_hbm(gate),
        in_hbm(up),
        in_hbm(mask),
        specs=[ANY] * 3,
        scratch=[pltpu.VMEM(gate.shape, BF16)] * 2
        + [pltpu.SMEM(mask.shape, jnp.int32), pltpu.SemaphoreType.DMA((3,))],
        after=after,
    )


def gradients(shares, dg, du, after=()):
    rows, cols = dg.shape
    n = len(shares)
    step = rows // 4

    def kernel(*refs):
        dg_ref, du_ref = refs[n : n + 2]
        out_g, out_u, token = refs[-3:]
        token[...] = jnp.zeros(token.shape, BF16)
        total = refs[0][...].astype(F32)
        for ref in refs[1:n]:
            total += ref[...].astype(F32)
        out_g[...] = (total * dg_ref[...]).astype(BF16)
        out_u[...] = (total * du_ref[...]).astype(BF16)

    block = pl.BlockSpec((step, cols), lambda i: (i, 0))
    return pl.pallas_call(
        kernel,
        grid=(rows // step,),
        in_specs=[block] * (n + 2) + [ANY] * len(after),
        out_specs=[block] * 2 + [VMEM],
        out_shape=[jax.ShapeDtypeStruct((rows, cols), BF16)] * 2
        + [pltpu.VMEM((16, 128), BF16)],
        compiler_params=PARAMS,
        name="gradients",
    )(*map(in_vmem, shares), in_vmem(dg), in_vmem(du), *after)


def stack(pieces, after=()):
    part, width = pieces[0].shape

    def kernel(*refs):
        for i in range(len(pieces)):
            refs[-1][i * part : (i + 1) * part, :] = refs[i][...]

    shape = (len(pieces) * part, width)
    return call(kernel, "stack", [(shape, BF16)], *map(in_vmem, pieces), after=after)[0]


def quarters(cot, chips):
    tok, width = cot.shape
    part = tok // chips

    def kernel(x_ref, *rest):
        outs, sem = rest[:chips], rest[chips]
        _, a, _ = place()
        copies = [
            pltpu.make_async_copy(
                x_ref.at[pl.ds(pl.multiple_of((a ^ u) * part, part), part)], outs[u], sem.at[u]
            )
            for u in range(chips)
        ]
        for copy in copies:
            copy.start()
        for copy in copies:
            copy.wait()

    return call(
        kernel,
        "quarters",
        [((part, width), BF16)] * chips,
        in_hbm(cot),
        specs=[ANY],
        scratch=[pltpu.SemaphoreType.DMA((chips,))],
    )


def choose(pieces, order, after=()):
    n = len(pieces)

    def kernel(*refs):
        r, a, _ = place()
        for i, t in enumerate(order):
            for u in range(n):

                @pl.when((r ^ a ^ t) == u)
                def _():
                    refs[n + i][...] = refs[u][...]

    shape = (pieces[0].shape, BF16)
    return call(kernel, "choose", [shape] * len(order), *map(in_vmem, pieces), after=after)


def back_product(own, other, weight, tok, after=()):
    chips = len(own)
    chunk, width = own[0].shape
    part = tok // chips
    blocks = chunk // part
    dr, ff = weight.shape
    step = 512

    def kernel(*refs):
        w_ref, c_ref, out2, out3 = refs[chips + 2 : chips + 6]
        _, a, h = place()
        for w in range(2):
            lanes = pl.ds(pl.multiple_of((h ^ w) * width, width), width)
            for u in range(chips):
                for t in range(blocks):
                    rows = pl.ds(pl.multiple_of(t * tok + (a ^ u) * part, part), part)
                    if w == 0:
                        c_ref[rows, lanes] = refs[u][t * part : (t + 1) * part, :]
                    else:
                        pair, at = ((0, 0), (1, 0), (1, 1), (0, 1))[u]
                        at = at * chunk + t * part
                        c_ref[rows, lanes] = refs[chips + pair][at : at + part, :]
        for j in range(0, ff, step):
            product = jnp.dot(
                c_ref[2 * tok : 4 * tok, :], w_ref[:, j : j + step], preferred_element_type=F32
            ).astype(BF16)
            out2[:, j : j + step] = product[:tok]
            out3[:, j : j + step] = product[tok:]

    return call(
        kernel,
        "back_product",
        [((blocks * tok, dr), BF16)] + [((tok, ff), BF16)] * 2,
        *map(in_vmem, own),
        *map(in_vmem, other),
        in_vmem(weight),
        after=after,
    )


def back_rest(cot, weight, tok, after=()):
    dr, ff = weight.shape
    step = 512

    def kernel(c_ref, w_ref, out0, out1):
        for j in range(0, ff, step):
            product = jnp.dot(
                c_ref[: 2 * tok, :], w_ref[:, j : j + step], preferred_element_type=F32
            ).astype(BF16)
            out0[:, j : j + step] = product[:tok]
            out1[:, j : j + step] = product[tok:]

    return call(
        kernel,
        "back_rest",
        [((tok, ff), BF16)] * 2,
        in_vmem(cot),
        in_vmem(weight),
        after=after,
    )


def out_product(hidden, pairs, weight, pieces, after=()):
    tok, ff = (*hidden, *map(lambda pair: pair[0], pairs))[0].shape
    half = weight.shape[0] // 2
    n = len(hidden)
    flat = [x for pair in pairs for x in pair]
    rows = (n + len(pairs)) * tok
    size = half // pieces
    step = min(size, 512)

    def kernel(*refs):
        w_ref = refs[n + len(flat)]
        outs = refs[n + len(flat) + 1 :]
        sent, own_ref, blocks = outs[:pieces], outs[pieces], outs[pieces + 1 :]
        _, _, h = place()
        for i in range(len(pairs)):
            blocks[i][...] = refs[n + 2 * i][...] + refs[n + 2 * i + 1][...]
        lhs = jnp.concatenate([ref[...] for ref in (*refs[:n], *blocks)], axis=0)
        for own, first in ((False, (1 - h) * half), (True, h * half)):
            for j in range(0, half, step):
                at = pl.ds(pl.multiple_of(first + j, step), step)
                product = lax.dot_general(
                    lhs, w_ref[at, :], (((1,), (1,)), ((), ())), preferred_element_type=F32
                )
                if own:
                    own_ref[:, j : j + step] = product
                else:
                    sent[j // size][:, j % size : j % size + step] = product.astype(BF16)

    return call(
        kernel,
        "out_product",
        [((rows, size), BF16)] * pieces
        + [((rows, half), F32)]
        + [((tok, ff), BF16)] * len(pairs),
        *map(in_vmem, hidden),
        *map(in_vmem, flat),
        in_vmem(weight),
        after=after,
    )


def add_and_pass(pairs, passed=(), after=()):
    flat = [x for pair in pairs for x in pair]

    def kernel(*refs):
        outs = refs[len(flat) + len(passed) :]
        for i in range(len(pairs)):
            outs[i][...] = (
                refs[2 * i][...].astype(F32) + refs[2 * i + 1][...].astype(F32)
            ).astype(BF16)
        for i in range(len(passed)):
            outs[len(pairs) + i][...] = refs[len(flat) + i][...]

    shapes = [(pair[0].shape, BF16) for pair in pairs] + [(x.shape, BF16) for x in passed]
    return call(
        kernel, "add_and_pass", shapes, *map(in_vmem, flat), *map(in_vmem, passed), after=after
    )


def pair_sum(owns, received, tok, chips, after=()):
    width = owns[0].shape[1]
    blocks = sum(own.shape[0] for own in owns) // tok
    part = tok // chips
    flat = [x for chunk in received for x in chunk]

    def kernel(*refs):
        outs = refs[len(owns) + len(flat) :]
        _, a, _ = place()
        to, at_piece = 0, len(owns)
        for i, chunk in enumerate(received):
            step = chunk[0].shape[1]
            for b in range(owns[i].shape[0] // tok):
                for u in range(chips):
                    at = pl.ds(pl.multiple_of(b * tok + (a ^ u) * part, part), part)
                    for j in range(len(chunk)):
                        lanes = slice(j * step, (j + 1) * step)
                        outs[u][to * part : (to + 1) * part, lanes] = (
                            refs[i][at, lanes] + refs[at_piece + j][at, :].astype(F32)
                        ).astype(BF16)
                to += 1
            at_piece += len(chunk)

    return call(
        kernel,
        "pair_sum",
        [((blocks * part, width), BF16)] * chips,
        *map(in_vmem, owns),
        *map(in_vmem, flat),
        after=after,
    )


def plane_sum(pieces, part, after=()):
    n = len(pieces)
    blocks = pieces[0].shape[0] // part

    def kernel(*refs):
        outs = refs[n:]
        r, a, _ = place()
        for t in range(blocks):
            at = slice(t * part, (t + 1) * part)
            total = refs[0][at, :].astype(F32)
            for ref in refs[1:n]:
                total += ref[at, :].astype(F32)
            total = total.astype(BF16)
            for k in range(blocks):

                @pl.when((r ^ a ^ k) == t)
                def _():
                    outs[k][...] = total

    shape = ((part, pieces[0].shape[1]), BF16)
    return call(kernel, "plane_sum", [shape] * blocks, *map(in_vmem, pieces), after=after)


def assemble(pieces, after=()):
    n = len(pieces)
    part, width = pieces[0].shape

    def kernel(*refs):
        r, _, _ = place()
        for k in range(n):
            refs[-1][pl.ds(pl.multiple_of((r ^ k) * part, part), part), :] = refs[k][...]

    return pl.pallas_call(
        kernel,
        in_specs=[VMEM] * n + [ANY] * len(after),
        out_specs=VMEM,
        out_shape=jax.ShapeDtypeStruct((n * part, width), BF16),
        compiler_params=PARAMS,
        name="assemble",
    )(*map(in_vmem, pieces), *after)


def down_gradient(cot, hidden, mask_rows, half, begun=None, after=()):
    n = len(hidden)
    tok, ff = hidden[0].shape
    tokens, dr = cot.shape
    tile_r = mask_rows.shape[0]
    size = dr // tile_r
    step = dr // 4
    extra = ([] if begun is None else [begun]) + list(after)

    def kernel(c_ref, *refs):
        m_ref = refs[n]
        o_ref, t_ref, h_ref = refs[-3:]
        i = pl.program_id(0)
        t_ref[...] = jnp.zeros(t_ref.shape, BF16)

        @pl.when(i == 0)
        def _():
            for t in range(n):
                h_ref[t * tok : (t + 1) * tok, :] = refs[t][...]

        product = lax.dot_general(
            c_ref[...], h_ref[...], (((0,), (0,)), ((), ())), preferred_element_type=F32
        )
        for b in range(step // size):
            kept = m_ref[pl.ds((2 * half + i) * (step // size) + b, 1), :] > 0
            at = slice(b * size, (b + 1) * size)
            o_ref[at, :] = jnp.where(kept, product[at, :], 0.0).astype(BF16)

    return pl.pallas_call(
        kernel,
        grid=(2,),
        in_specs=[pl.BlockSpec((tokens, step), lambda i: (0, 2 * half + i))]
        + [VMEM] * (n + 1)
        + [ANY] * len(extra),
        out_specs=[pl.BlockSpec((step, ff), lambda i: (2 * half + i, 0)), VMEM],
        out_shape=[jax.ShapeDtypeStruct((dr, ff), BF16), pltpu.VMEM((16, 128), BF16)],
        scratch_shapes=[pltpu.VMEM((tokens, ff), BF16)],
        input_output_aliases={} if begun is None else {n + 2: 0},
        compiler_params=PARAMS,
        cost_estimate=pl.CostEstimate(
            flops=0, bytes_accessed=0, transcendentals=0
        ),
        name="down_gradient",
    )(in_vmem(cot), *map(in_vmem, hidden), in_vmem(mask_rows), *extra)


def fast_body(gate_pre, up_pre, down_weight, block_mask, cotangent):
    rows, chips = 4, 4
    tok = gate_pre.shape[0]
    part = tok // chips

    def over_row(x, t, senders=range(4)):
        return lax.ppermute(x, "row", [(i, i ^ t) for i in senders])

    def over_chips(x, u):
        return lax.ppermute(x, "col", [(j, j ^ (2 * u)) for j in range(2 * chips)])

    def over_core(x):
        return lax.ppermute(x, "col", [(j, j ^ 1) for j in range(2 * chips)])

    ends, inner = (0, 3), (1, 2)

    mine = quarters(cotangent, chips)
    spread = [mine[0]] + [over_chips(mine[u], u) for u in range(1, chips)]
    first, dg, du, mask_rows = gated(
        gate_pre, up_pre, block_mask, down_weight.shape[1], after=[mine[0]]
    )
    weight = masked_weight(down_weight, mask_rows, 0, after=[first])
    ours = choose(spread, (3, 2, 1, 0), after=[weight])
    cot = {t: over_row(x, t) for t, x in zip((3, 2, 1), ours)}
    cot[0] = ours[3]
    weight = masked_weight(down_weight, mask_rows, 1, weight, after=[ours[0]])

    mine = stack([cot[t] for t in range(rows)], after=[weight])
    same = [mine] + [over_chips(mine, u) for u in range(1, chips)]

    hidden = {0: add_and_pass([], [first], after=[mine])[0]}
    hidden[1] = over_row(hidden[0], 1)
    inner3 = over_row(hidden[0], 3, inner)
    inner2 = over_row(hidden[1], 3, inner)
    ends2 = over_row(inner3, 1, inner)

    other = [over_core(stack([same[0], same[3]])), over_core(stack([same[1], same[2]]))]
    cot, back2, back3 = back_product(same, other, weight, tok, after=[hidden[1], inner3])

    first3 = over_row(back3, 1, ends)
    first2 = over_row(back2, 1, ends)
    hidden[2], inner2 = add_and_pass([(inner2, ends2)], [inner2], after=[back3])
    ends3 = over_row(inner2, 1, inner)
    (to_pass,) = add_and_pass([(back2, first3)], after=[inner2])
    second = over_row(to_pass, 3, inner)
    back0, back1 = back_rest(cot, weight, tok, after=[to_pass])

    *sent, own01 = out_product([hidden[0], hidden[1]], [], weight, 2, after=[back1, to_pass])
    received = [[over_core(x) for x in sent]]
    *sent, own23, hidden[3] = out_product(
        [hidden[2]], [[inner3, ends3]], weight, 2, after=[own01]
    )
    received.append([over_core(x) for x in sent])
    to_inner, to_near = add_and_pass([(back3, first2), (back1, second)], after=[own23])
    across = over_row(to_inner, 3, inner)
    beside = over_row(to_near, 1)
    pieces = pair_sum([own01, own23], received, tok, chips)
    pieces = [pieces[0]] + [over_chips(pieces[u], u) for u in range(1, chips)]
    tokens = [hidden[t] for t in range(rows)]
    d_down, done = down_gradient(cot, tokens, mask_rows, 0, after=[pieces[0]])
    d_down, done = down_gradient(cot, tokens, mask_rows, 1, d_down, after=[done])
    ready = plane_sum(pieces, part, after=[done])
    d_gate, d_up, last = gradients([back0, beside, across], dg, du, after=[ready[0]])

    width = 2 * chips
    placed = [
        lax.ppermute(
            ready[k],
            ("row", "col"),
            [
                (r * width + 2 * a + h, (a ^ k) * width + 2 * r + h)
                for r in range(rows)
                for a in range(chips)
                for h in range(2)
            ],
        )
        for k in range(rows)
    ]
    output = assemble(placed, after=[last])

    return output, d_gate, d_up, d_down


def rounded_f32(values):
    return lax.optimization_barrier(values.astype(BF16)).astype(F32)


def general_body(gate_pre, up_pre, down_weight, block_mask, cotangent):
    tok_rows, ff_cols = gate_pre.shape
    d_rows = down_weight.shape[0]
    block_size = d_rows // block_mask.shape[0]
    gate_wide = gate_pre.astype(F32)
    up_wide = up_pre.astype(F32)
    activated = jax.nn.silu(gate_wide)
    hidden = (activated * up_wide).astype(BF16)
    expand = jnp.repeat(jnp.repeat(block_mask, block_size, axis=0), block_size, axis=1)
    masked = jnp.where(expand > 0, down_weight, jnp.zeros_like(down_weight))
    cot_row = lax.all_gather(cotangent, "col", axis=1, tiled=True)
    cot_all = lax.all_to_all(cot_row, "row", split_axis=1, concat_axis=0, tiled=True)
    panel = lax.all_gather(masked, "row", axis=0, tiled=True)
    y_partial = lax.dot_general(
        hidden, panel, (((1,), (1,)), ((), ())), preferred_element_type=F32
    )
    shards = panel.shape[0] // d_rows
    per_shard = jnp.einsum(
        "tnd,ndf->ntf",
        cot_row.reshape(tok_rows, shards, d_rows),
        panel.reshape(shards, d_rows, ff_cols),
        preferred_element_type=F32,
    )
    d_hidden = jnp.sum(rounded_f32(per_shard), axis=0)
    hidden_all = lax.all_gather(hidden, "row", axis=0, tiled=True)
    grad_full = lax.dot_general(
        cot_all, hidden_all, (((0,), (0,)), ((), ())), preferred_element_type=F32
    )
    output = lax.psum_scatter(y_partial.astype(BF16), "col", scatter_dimension=1, tiled=True)
    sigmoid_g = jax.nn.sigmoid(gate_wide)
    d_gate = (d_hidden * up_wide * sigmoid_g * (1.0 + gate_wide * (1.0 - sigmoid_g))).astype(BF16)
    d_up = (d_hidden * activated).astype(BF16)
    d_down = jnp.where(expand > 0, grad_full, jnp.zeros_like(grad_full)).astype(BF16)
    return output, d_gate, d_up, d_down


def solution(mesh):
    spec = P("row", "col")
    small = mesh.shape["row"] == 4 and mesh.shape["col"] == 8
    return jax.shard_map(
        fast_body if small else general_body,
        mesh=mesh,
        in_specs=(spec,) * 5,
        out_specs=(spec,) * 4,
        check_vma=False,
    )
```

```python
import jax
import jax.numpy as jnp
from jax import lax
from jax.experimental import pallas as pl
from jax.experimental.pallas import tpu as pltpu
from jax.sharding import PartitionSpec as P

F32 = jnp.float32
BF16 = jnp.bfloat16
VMEM = pl.BlockSpec(memory_space=pltpu.VMEM)
SMEM = pl.BlockSpec(memory_space=pltpu.SMEM)
PARAMS = pltpu.CompilerParams(vmem_limit_bytes=16 * 2**20)


ANY = pl.BlockSpec(memory_space=pl.ANY)


def in_vmem(array):
    return pltpu.with_memory_space_constraint(array, pltpu.VMEM)


def in_hbm(array):
    return pltpu.with_memory_space_constraint(array, pltpu.HBM)


def place():
    col = lax.axis_index("col")
    return lax.axis_index("row"), col // 2, col % 2


COSTS = {'quarters': 311445000, 'gated': 588285000, 'masked_weight': 761310000, 'choose': 34605000, 'stack': 34605000, 'back_product': 865125000, 'back_rest': 830520000, 'out_product': 830520000, 'pair_sum': 69210000, 'plane_sum': 3460500000, 'add_and_pass': 69210000, 'down_gradient': 1418804999, 'gradients': 588285000, 'assemble': 242235000, 'to_vmem': 311445000}


def call(kernel, name, outs, *args, specs=None, scratch=(), flops=0, moved=0, after=()):
    n, m = len(args), len(args) + len(after)

    def body(*refs):
        kernel(*refs[:n], *refs[m:])

    return pl.pallas_call(
        body,
        in_specs=(specs or [VMEM] * n) + [pl.BlockSpec(memory_space=pl.ANY)] * len(after),
        out_specs=[VMEM] * len(outs),
        out_shape=[pltpu.VMEM(shape, dtype) for shape, dtype in outs],
        scratch_shapes=list(scratch),
        compiler_params=PARAMS,
        cost_estimate=pl.CostEstimate(flops=COSTS[name], bytes_accessed=0, transcendentals=0),
        name=name,
    )(*args, *after)


def masked_weight(weight, mask_rows, half, begun=None, after=()):
    rows, cols = weight.shape
    tile_r = mask_rows.shape[0]
    size = rows // tile_r
    mine = range(half * tile_r // 2, (half + 1) * tile_r // 2)
    extra = [] if begun is None else [in_vmem(begun)]

    def kernel(w_ref, m_ref, *refs):
        o_ref, sem = refs[-2:]

        def copy(i):
            at = pl.ds(i * size, size)
            return pltpu.make_async_copy(w_ref.at[at], o_ref.at[at], sem.at[i - mine[0]])

        for i in mine:
            copy(i).start()
        for i in mine:
            copy(i).wait()
            at = slice(i * size, (i + 1) * size)
            o_ref[at, :] = jnp.where(m_ref[i : i + 1, :] > 0, o_ref[at, :], jnp.zeros((), BF16))

    return pl.pallas_call(
        kernel,
        in_specs=[ANY, VMEM] + [VMEM] * len(extra) + [ANY] * len(after),
        out_specs=VMEM,
        out_shape=pltpu.VMEM((rows, cols), BF16),
        input_output_aliases={} if begun is None else {2: 0},
        scratch_shapes=[pltpu.SemaphoreType.DMA((len(mine),))],
        compiler_params=PARAMS,
        cost_estimate=pl.CostEstimate(flops=COSTS["masked_weight"], bytes_accessed=0, transcendentals=0),
        name="masked_weight",
    )(in_hbm(weight), in_vmem(mask_rows), *extra, *after)


def gated(gate, up, mask, width, after=()):
    tile_r, tile_c = mask.shape
    size = width // tile_c

    def kernel(g_hbm, u_hbm, m_hbm, o_ref, dg_ref, du_ref, rows_ref, g_ref, u_ref, m_ref, sem):
        copies = [
            pltpu.make_async_copy(m_hbm, m_ref, sem.at[2]),
            pltpu.make_async_copy(g_hbm, g_ref, sem.at[0]),
            pltpu.make_async_copy(u_hbm, u_ref, sem.at[1]),
        ]
        for copy in copies:
            copy.start()
        copies[0].wait()
        for i in range(tile_r):
            for j in range(tile_c):
                rows_ref[i : i + 1, j * size : (j + 1) * size] = jnp.full(
                    (1, size), m_ref[i, j], jnp.int32
                )
        for copy in copies[1:]:
            copy.wait()
        g = g_ref[...].astype(F32)
        u = u_ref[...].astype(F32)
        s = 1.0 / (1.0 + jnp.exp(-g))
        o_ref[...] = (g * s * u).astype(BF16)
        dg_ref[...] = u * s * (1.0 + g * (1.0 - s))
        du_ref[...] = g * s

    return call(
        kernel,
        "gated",
        [
            (gate.shape, BF16),
            (gate.shape, F32),
            (gate.shape, F32),
            ((tile_r, width), jnp.int32),
        ],
        in_hbm(gate),
        in_hbm(up),
        in_hbm(mask),
        specs=[ANY] * 3,
        scratch=[pltpu.VMEM(gate.shape, BF16)] * 2
        + [pltpu.SMEM(mask.shape, jnp.int32), pltpu.SemaphoreType.DMA((3,))],
        after=after,
    )


def gradients(shares, dg, du, after=()):
    rows, cols = dg.shape
    n = len(shares)
    step = rows // 4

    def kernel(*refs):
        dg_ref, du_ref = refs[n : n + 2]
        out_g, out_u, token = refs[-3:]
        token[...] = jnp.zeros(token.shape, BF16)
        total = refs[0][...].astype(F32)
        for ref in refs[1:n]:
            total += ref[...].astype(F32)
        out_g[...] = (total * dg_ref[...]).astype(BF16)
        out_u[...] = (total * du_ref[...]).astype(BF16)

    block = pl.BlockSpec((step, cols), lambda i: (i, 0))
    return pl.pallas_call(
        kernel,
        grid=(rows // step,),
        in_specs=[block] * (n + 2) + [ANY] * len(after),
        out_specs=[block] * 2 + [VMEM],
        out_shape=[jax.ShapeDtypeStruct((rows, cols), BF16)] * 2
        + [pltpu.VMEM((16, 128), BF16)],
        compiler_params=PARAMS,
        cost_estimate=pl.CostEstimate(flops=COSTS["gradients"], bytes_accessed=0, transcendentals=0),
        name="gradients",
    )(*map(in_vmem, shares), in_vmem(dg), in_vmem(du), *after)


def stack(pieces, after=()):
    part, width = pieces[0].shape

    def kernel(*refs):
        for i in range(len(pieces)):
            refs[-1][i * part : (i + 1) * part, :] = refs[i][...]

    shape = (len(pieces) * part, width)
    return call(kernel, "stack", [(shape, BF16)], *map(in_vmem, pieces), after=after)[0]


def quarters(cot, chips):
    tok, width = cot.shape
    part = tok // chips

    def kernel(x_ref, *rest):
        outs, sem = rest[:chips], rest[chips]
        _, a, _ = place()
        copies = [
            pltpu.make_async_copy(
                x_ref.at[pl.ds(pl.multiple_of((a ^ u) * part, part), part)], outs[u], sem.at[u]
            )
            for u in range(chips)
        ]
        for copy in copies:
            copy.start()
        for copy in copies:
            copy.wait()

    return call(
        kernel,
        "quarters",
        [((part, width), BF16)] * chips,
        in_hbm(cot),
        specs=[ANY],
        scratch=[pltpu.SemaphoreType.DMA((chips,))],
    )


def choose(pieces, order, after=()):
    n = len(pieces)

    def kernel(*refs):
        r, a, _ = place()
        for i, t in enumerate(order):
            for u in range(n):

                @pl.when((r ^ a ^ t) == u)
                def _():
                    refs[n + i][...] = refs[u][...]

    shape = (pieces[0].shape, BF16)
    return call(kernel, "choose", [shape] * len(order), *map(in_vmem, pieces), after=after)


def back_product(own, other, weight, tok, after=()):
    chips = len(own)
    chunk, width = own[0].shape
    part = tok // chips
    blocks = chunk // part
    dr, ff = weight.shape
    step = 512

    def kernel(*refs):
        w_ref, c_ref, out2, out3 = refs[chips + 2 : chips + 6]
        _, a, h = place()
        for w in range(2):
            lanes = pl.ds(pl.multiple_of((h ^ w) * width, width), width)
            for u in range(chips):
                for t in range(blocks):
                    rows = pl.ds(pl.multiple_of(t * tok + (a ^ u) * part, part), part)
                    if w == 0:
                        c_ref[rows, lanes] = refs[u][t * part : (t + 1) * part, :]
                    else:
                        pair, at = ((0, 0), (1, 0), (1, 1), (0, 1))[u]
                        at = at * chunk + t * part
                        c_ref[rows, lanes] = refs[chips + pair][at : at + part, :]
        for j in range(0, ff, step):
            product = jnp.dot(
                c_ref[2 * tok : 4 * tok, :], w_ref[:, j : j + step], preferred_element_type=F32
            ).astype(BF16)
            out2[:, j : j + step] = product[:tok]
            out3[:, j : j + step] = product[tok:]

    return call(
        kernel,
        "back_product",
        [((blocks * tok, dr), BF16)] + [((tok, ff), BF16)] * 2,
        *map(in_vmem, own),
        *map(in_vmem, other),
        in_vmem(weight),
        after=after,
    )


def back_rest(cot, weight, tok, after=()):
    dr, ff = weight.shape
    step = 512

    def kernel(c_ref, w_ref, out0, out1):
        for j in range(0, ff, step):
            product = jnp.dot(
                c_ref[: 2 * tok, :], w_ref[:, j : j + step], preferred_element_type=F32
            ).astype(BF16)
            out0[:, j : j + step] = product[:tok]
            out1[:, j : j + step] = product[tok:]

    return call(
        kernel,
        "back_rest",
        [((tok, ff), BF16)] * 2,
        in_vmem(cot),
        in_vmem(weight),
        after=after,
    )


def out_product(hidden, pairs, weight, pieces, after=()):
    tok, ff = (*hidden, *map(lambda pair: pair[0], pairs))[0].shape
    half = weight.shape[0] // 2
    n = len(hidden)
    flat = [x for pair in pairs for x in pair]
    rows = (n + len(pairs)) * tok
    size = half // pieces
    step = min(size, 512)

    def kernel(*refs):
        w_ref = refs[n + len(flat)]
        outs = refs[n + len(flat) + 1 :]
        sent, own_ref, blocks = outs[:pieces], outs[pieces], outs[pieces + 1 :]
        _, _, h = place()
        for i in range(len(pairs)):
            blocks[i][...] = refs[n + 2 * i][...] + refs[n + 2 * i + 1][...]
        lhs = jnp.concatenate([ref[...] for ref in (*refs[:n], *blocks)], axis=0)
        for own, first in ((False, (1 - h) * half), (True, h * half)):
            for j in range(0, half, step):
                at = pl.ds(pl.multiple_of(first + j, step), step)
                product = lax.dot_general(
                    lhs, w_ref[at, :], (((1,), (1,)), ((), ())), preferred_element_type=F32
                )
                if own:
                    own_ref[:, j : j + step] = product
                else:
                    sent[j // size][:, j % size : j % size + step] = product.astype(BF16)

    return call(
        kernel,
        "out_product",
        [((rows, size), BF16)] * pieces
        + [((rows, half), F32)]
        + [((tok, ff), BF16)] * len(pairs),
        *map(in_vmem, hidden),
        *map(in_vmem, flat),
        in_vmem(weight),
        after=after,
    )


def add_and_pass(pairs, passed=(), after=()):
    flat = [x for pair in pairs for x in pair]

    def kernel(*refs):
        outs = refs[len(flat) + len(passed) :]
        for i in range(len(pairs)):
            outs[i][...] = (
                refs[2 * i][...].astype(F32) + refs[2 * i + 1][...].astype(F32)
            ).astype(BF16)
        for i in range(len(passed)):
            outs[len(pairs) + i][...] = refs[len(flat) + i][...]

    shapes = [(pair[0].shape, BF16) for pair in pairs] + [(x.shape, BF16) for x in passed]
    return call(
        kernel, "add_and_pass", shapes, *map(in_vmem, flat), *map(in_vmem, passed), after=after
    )


def pair_sum(owns, received, tok, chips, after=()):
    width = owns[0].shape[1]
    blocks = sum(own.shape[0] for own in owns) // tok
    part = tok // chips
    flat = [x for chunk in received for x in chunk]

    def kernel(*refs):
        outs = refs[len(owns) + len(flat) :]
        _, a, _ = place()
        to, at_piece = 0, len(owns)
        for i, chunk in enumerate(received):
            step = chunk[0].shape[1]
            for b in range(owns[i].shape[0] // tok):
                for u in range(chips):
                    at = pl.ds(pl.multiple_of(b * tok + (a ^ u) * part, part), part)
                    for j in range(len(chunk)):
                        lanes = slice(j * step, (j + 1) * step)
                        outs[u][to * part : (to + 1) * part, lanes] = (
                            refs[i][at, lanes] + refs[at_piece + j][at, :].astype(F32)
                        ).astype(BF16)
                to += 1
            at_piece += len(chunk)

    return call(
        kernel,
        "pair_sum",
        [((blocks * part, width), BF16)] * chips,
        *map(in_vmem, owns),
        *map(in_vmem, flat),
        after=after,
    )


def plane_sum(pieces, part, after=()):
    n = len(pieces)
    blocks = pieces[0].shape[0] // part

    def kernel(*refs):
        outs = refs[n:]
        r, a, _ = place()
        for t in range(blocks):
            at = slice(t * part, (t + 1) * part)
            total = refs[0][at, :].astype(F32)
            for ref in refs[1:n]:
                total += ref[at, :].astype(F32)
            total = total.astype(BF16)
            for k in range(blocks):

                @pl.when((r ^ a ^ k) == t)
                def _():
                    outs[k][...] = total

    shape = ((part, pieces[0].shape[1]), BF16)
    return call(kernel, "plane_sum", [shape] * blocks, *map(in_vmem, pieces), after=after)


def assemble(pieces, after=()):
    n = len(pieces)
    part, width = pieces[0].shape

    def kernel(*refs):
        r, _, _ = place()
        for k in range(n):
            refs[-1][pl.ds(pl.multiple_of((r ^ k) * part, part), part), :] = refs[k][...]

    return pl.pallas_call(
        kernel,
        in_specs=[VMEM] * n + [ANY] * len(after),
        out_specs=VMEM,
        out_shape=jax.ShapeDtypeStruct((n * part, width), BF16),
        compiler_params=PARAMS,
        cost_estimate=pl.CostEstimate(flops=COSTS["assemble"], bytes_accessed=0, transcendentals=0),
        name="assemble",
    )(*map(in_vmem, pieces), *after)


def down_gradient(cot, hidden, mask_rows, half, begun=None, after=()):
    n = len(hidden)
    tok, ff = hidden[0].shape
    tokens, dr = cot.shape
    tile_r = mask_rows.shape[0]
    size = dr // tile_r
    step = dr // 4
    extra = ([] if begun is None else [begun]) + list(after)

    def kernel(c_ref, *refs):
        m_ref = refs[n]
        o_ref, t_ref, h_ref = refs[-3:]
        i = pl.program_id(0)
        t_ref[...] = jnp.zeros(t_ref.shape, BF16)

        @pl.when(i == 0)
        def _():
            for t in range(n):
                h_ref[t * tok : (t + 1) * tok, :] = refs[t][...]

        product = lax.dot_general(
            c_ref[...], h_ref[...], (((0,), (0,)), ((), ())), preferred_element_type=F32
        )
        for b in range(step // size):
            kept = m_ref[pl.ds((2 * half + i) * (step // size) + b, 1), :] > 0
            at = slice(b * size, (b + 1) * size)
            o_ref[at, :] = jnp.where(kept, product[at, :], 0.0).astype(BF16)

    return pl.pallas_call(
        kernel,
        grid=(2,),
        in_specs=[pl.BlockSpec((tokens, step), lambda i: (0, 2 * half + i))]
        + [VMEM] * (n + 1)
        + [ANY] * len(extra),
        out_specs=[pl.BlockSpec((step, ff), lambda i: (2 * half + i, 0)), VMEM],
        out_shape=[jax.ShapeDtypeStruct((dr, ff), BF16), pltpu.VMEM((16, 128), BF16)],
        scratch_shapes=[pltpu.VMEM((tokens, ff), BF16)],
        input_output_aliases={} if begun is None else {n + 2: 0},
        compiler_params=PARAMS,
        cost_estimate=pl.CostEstimate(flops=COSTS["down_gradient"], bytes_accessed=0, transcendentals=0),
        name="down_gradient",
    )(in_vmem(cot), *map(in_vmem, hidden), in_vmem(mask_rows), *extra)


def fast_body(gate_pre, up_pre, down_weight, block_mask, cotangent):
    rows, chips = 4, 4
    tok = gate_pre.shape[0]
    part = tok // chips

    def over_row(x, t, senders=range(4)):
        return lax.ppermute(x, "row", [(i, i ^ t) for i in senders])

    def over_chips(x, u):
        return lax.ppermute(x, "col", [(j, j ^ (2 * u)) for j in range(2 * chips)])

    def over_core(x):
        return lax.ppermute(x, "col", [(j, j ^ 1) for j in range(2 * chips)])

    ends, inner = (0, 3), (1, 2)

    mine = quarters(cotangent, chips)
    spread = [mine[0]] + [over_chips(mine[u], u) for u in range(1, chips)]
    first, dg, du, mask_rows = gated(
        gate_pre, up_pre, block_mask, down_weight.shape[1], after=[mine[0]]
    )
    weight = masked_weight(down_weight, mask_rows, 0, after=[first])
    ours = choose(spread, (3, 2, 1, 0), after=[weight])
    cot = {t: over_row(x, t) for t, x in zip((3, 2, 1), ours)}
    cot[0] = ours[3]
    weight = masked_weight(down_weight, mask_rows, 1, weight, after=[ours[0]])

    mine = stack([cot[t] for t in range(rows)], after=[weight])
    same = [mine] + [over_chips(mine, u) for u in range(1, chips)]

    hidden = {0: add_and_pass([], [first], after=[mine])[0]}
    hidden[1] = over_row(hidden[0], 1)
    inner3 = over_row(hidden[0], 3, inner)
    inner2 = over_row(hidden[1], 3, inner)
    ends2 = over_row(inner3, 1, inner)

    other = [over_core(stack([same[0], same[3]])), over_core(stack([same[1], same[2]]))]
    cot, back2, back3 = back_product(same, other, weight, tok, after=[hidden[1], inner3])

    first3 = over_row(back3, 1, ends)
    first2 = over_row(back2, 1, ends)
    *sent, own01 = out_product([hidden[0], hidden[1]], [], weight, 1, after=[back3])
    received = [[over_core(x) for x in sent]]
    back0, back1 = back_rest(cot, weight, tok, after=[own01])
    (inner2,) = add_and_pass([], [inner2], after=[back1])
    ends3 = over_row(inner2, 1, inner)
    (hidden[2],) = add_and_pass([(inner2, ends2)], after=[inner2])
    (to_pass,) = add_and_pass([(back2, first3)], after=[hidden[2]])
    second = over_row(to_pass, 3, inner)
    *sent, own23, hidden[3] = out_product(
        [hidden[2]], [[inner3, ends3]], weight, 2, after=[to_pass]
    )
    received.append([over_core(x) for x in sent])
    pieces = pair_sum([own01, own23], received, tok, chips)
    pieces = [pieces[0]] + [over_chips(pieces[u], u) for u in range(1, chips)]
    to_inner, to_near = add_and_pass([(back3, first2), (back1, second)], after=[pieces[0]])
    across = over_row(to_inner, 3, inner)
    beside = over_row(to_near, 1)
    tokens = [hidden[t] for t in range(rows)]
    d_down, done = down_gradient(cot, tokens, mask_rows, 0, after=[to_inner])
    d_down, done = down_gradient(cot, tokens, mask_rows, 1, d_down, after=[done])
    ready = plane_sum(pieces, part, after=[done])
    d_gate, d_up, last = gradients([back0, beside, across], dg, du, after=[ready[0]])

    width = 2 * chips
    placed = [
        lax.ppermute(
            ready[k],
            ("row", "col"),
            [
                (r * width + 2 * a + h, (a ^ k) * width + 2 * r + h)
                for r in range(rows)
                for a in range(chips)
                for h in range(2)
            ],
        )
        for k in range(rows)
    ]
    output = assemble(placed, after=[last])

    return output, d_gate, d_up, d_down


def rounded_f32(values):
    return lax.optimization_barrier(values.astype(BF16)).astype(F32)


def general_body(gate_pre, up_pre, down_weight, block_mask, cotangent):
    tok_rows, ff_cols = gate_pre.shape
    d_rows = down_weight.shape[0]
    block_size = d_rows // block_mask.shape[0]
    gate_wide = gate_pre.astype(F32)
    up_wide = up_pre.astype(F32)
    activated = jax.nn.silu(gate_wide)
    hidden = (activated * up_wide).astype(BF16)
    expand = jnp.repeat(jnp.repeat(block_mask, block_size, axis=0), block_size, axis=1)
    masked = jnp.where(expand > 0, down_weight, jnp.zeros_like(down_weight))
    cot_row = lax.all_gather(cotangent, "col", axis=1, tiled=True)
    cot_all = lax.all_to_all(cot_row, "row", split_axis=1, concat_axis=0, tiled=True)
    panel = lax.all_gather(masked, "row", axis=0, tiled=True)
    y_partial = lax.dot_general(
        hidden, panel, (((1,), (1,)), ((), ())), preferred_element_type=F32
    )
    shards = panel.shape[0] // d_rows
    per_shard = jnp.einsum(
        "tnd,ndf->ntf",
        cot_row.reshape(tok_rows, shards, d_rows),
        panel.reshape(shards, d_rows, ff_cols),
        preferred_element_type=F32,
    )
    d_hidden = jnp.sum(rounded_f32(per_shard), axis=0)
    hidden_all = lax.all_gather(hidden, "row", axis=0, tiled=True)
    grad_full = lax.dot_general(
        cot_all, hidden_all, (((0,), (0,)), ((), ())), preferred_element_type=F32
    )
    output = lax.psum_scatter(y_partial.astype(BF16), "col", scatter_dimension=1, tiled=True)
    sigmoid_g = jax.nn.sigmoid(gate_wide)
    d_gate = (d_hidden * up_wide * sigmoid_g * (1.0 + gate_wide * (1.0 - sigmoid_g))).astype(BF16)
    d_up = (d_hidden * activated).astype(BF16)
    d_down = jnp.where(expand > 0, grad_full, jnp.zeros_like(grad_full)).astype(BF16)
    return output, d_gate, d_up, d_down


def solution(mesh):
    spec = P("row", "col")
    small = mesh.shape["row"] == 4 and mesh.shape["col"] == 8
    return jax.shard_map(
        fast_body if small else general_body,
        mesh=mesh,
        in_specs=(spec,) * 5,
        out_specs=(spec,) * 4,
        check_vma=False,
    )
```

```python
import jax
import jax.numpy as jnp
from jax import lax
from jax.experimental import pallas as pl
from jax.experimental.pallas import tpu as pltpu
from jax.sharding import PartitionSpec as P

F32 = jnp.float32
BF16 = jnp.bfloat16
VMEM = pl.BlockSpec(memory_space=pltpu.VMEM)
SMEM = pl.BlockSpec(memory_space=pltpu.SMEM)
PARAMS = pltpu.CompilerParams(vmem_limit_bytes=16 * 2**20)


ANY = pl.BlockSpec(memory_space=pl.ANY)


def in_vmem(array):
    return pltpu.with_memory_space_constraint(array, pltpu.VMEM)


def in_hbm(array):
    return pltpu.with_memory_space_constraint(array, pltpu.HBM)


def place():
    col = lax.axis_index("col")
    return lax.axis_index("row"), col // 2, col % 2


COSTS = {'quarters': 311445000, 'gated': 588285000, 'masked_weight': 761310000, 'choose': 34605000, 'stack': 34605000, 'back_product': 865125000, 'back_rest': 830520000, 'out_product': 830520000, 'pair_sum': 69210000, 'plane_sum': 3460500000, 'add_and_pass': 69210000, 'down_gradient': 1418804999, 'gradients': 588285000, 'assemble': 242235000, 'to_vmem': 311445000}


def call(kernel, name, outs, *args, specs=None, scratch=(), flops=0, moved=0, after=()):
    n, m = len(args), len(args) + len(after)

    def body(*refs):
        kernel(*refs[:n], *refs[m:])

    return pl.pallas_call(
        body,
        in_specs=(specs or [VMEM] * n) + [pl.BlockSpec(memory_space=pl.ANY)] * len(after),
        out_specs=[VMEM] * len(outs),
        out_shape=[pltpu.VMEM(shape, dtype) for shape, dtype in outs],
        scratch_shapes=list(scratch),
        compiler_params=PARAMS,
        cost_estimate=pl.CostEstimate(flops=COSTS[name], bytes_accessed=0, transcendentals=0),
        name=name,
    )(*args, *after)


def masked_weight(weight, mask_rows, half, begun=None, after=()):
    rows, cols = weight.shape
    tile_r = mask_rows.shape[0]
    size = rows // tile_r
    mine = range(half * tile_r // 2, (half + 1) * tile_r // 2)
    extra = [] if begun is None else [in_vmem(begun)]

    def kernel(w_ref, m_ref, *refs):
        o_ref, sem = refs[-2:]

        def copy(i):
            at = pl.ds(i * size, size)
            return pltpu.make_async_copy(w_ref.at[at], o_ref.at[at], sem.at[i - mine[0]])

        for i in mine:
            copy(i).start()
        for i in mine:
            copy(i).wait()
            at = slice(i * size, (i + 1) * size)
            o_ref[at, :] = jnp.where(m_ref[i : i + 1, :] > 0, o_ref[at, :], jnp.zeros((), BF16))

    return pl.pallas_call(
        kernel,
        in_specs=[ANY, VMEM] + [VMEM] * len(extra) + [ANY] * len(after),
        out_specs=VMEM,
        out_shape=pltpu.VMEM((rows, cols), BF16),
        input_output_aliases={} if begun is None else {2: 0},
        scratch_shapes=[pltpu.SemaphoreType.DMA((len(mine),))],
        compiler_params=PARAMS,
        cost_estimate=pl.CostEstimate(flops=COSTS["masked_weight"], bytes_accessed=0, transcendentals=0),
        name="masked_weight",
    )(in_hbm(weight), in_vmem(mask_rows), *extra, *after)


def gated(gate, up, mask, width, after=()):
    tile_r, tile_c = mask.shape
    size = width // tile_c

    def kernel(g_hbm, u_hbm, m_hbm, o_ref, dg_ref, du_ref, rows_ref, g_ref, u_ref, m_ref, sem):
        copies = [
            pltpu.make_async_copy(m_hbm, m_ref, sem.at[2]),
            pltpu.make_async_copy(g_hbm, g_ref, sem.at[0]),
            pltpu.make_async_copy(u_hbm, u_ref, sem.at[1]),
        ]
        for copy in copies:
            copy.start()
        copies[0].wait()
        for i in range(tile_r):
            for j in range(tile_c):
                rows_ref[i : i + 1, j * size : (j + 1) * size] = jnp.full(
                    (1, size), m_ref[i, j], jnp.int32
                )
        for copy in copies[1:]:
            copy.wait()
        g = g_ref[...].astype(F32)
        u = u_ref[...].astype(F32)
        s = 1.0 / (1.0 + jnp.exp(-g))
        o_ref[...] = (g * s * u).astype(BF16)
        dg_ref[...] = u * s * (1.0 + g * (1.0 - s))
        du_ref[...] = g * s

    return call(
        kernel,
        "gated",
        [
            (gate.shape, BF16),
            (gate.shape, F32),
            (gate.shape, F32),
            ((tile_r, width), jnp.int32),
        ],
        in_hbm(gate),
        in_hbm(up),
        in_hbm(mask),
        specs=[ANY] * 3,
        scratch=[pltpu.VMEM(gate.shape, BF16)] * 2
        + [pltpu.SMEM(mask.shape, jnp.int32), pltpu.SemaphoreType.DMA((3,))],
        after=after,
    )


def gradients(shares, dg, du, after=()):
    rows, cols = dg.shape
    n = len(shares)
    step = rows // 4

    def kernel(*refs):
        dg_ref, du_ref = refs[n : n + 2]
        out_g, out_u, token = refs[-3:]
        token[...] = jnp.zeros(token.shape, BF16)
        total = refs[0][...].astype(F32)
        for ref in refs[1:n]:
            total += ref[...].astype(F32)
        out_g[...] = (total * dg_ref[...]).astype(BF16)
        out_u[...] = (total * du_ref[...]).astype(BF16)

    block = pl.BlockSpec((step, cols), lambda i: (i, 0))
    return pl.pallas_call(
        kernel,
        grid=(rows // step,),
        in_specs=[block] * (n + 2) + [ANY] * len(after),
        out_specs=[block] * 2 + [VMEM],
        out_shape=[jax.ShapeDtypeStruct((rows, cols), BF16)] * 2
        + [pltpu.VMEM((16, 128), BF16)],
        compiler_params=PARAMS,
        cost_estimate=pl.CostEstimate(flops=COSTS["gradients"], bytes_accessed=0, transcendentals=0),
        name="gradients",
    )(*map(in_vmem, shares), in_vmem(dg), in_vmem(du), *after)


def stack(pieces, after=()):
    part, width = pieces[0].shape

    def kernel(*refs):
        for i in range(len(pieces)):
            refs[-1][i * part : (i + 1) * part, :] = refs[i][...]

    shape = (len(pieces) * part, width)
    return call(kernel, "stack", [(shape, BF16)], *map(in_vmem, pieces), after=after)[0]


def quarters(cot, chips):
    tok, width = cot.shape
    part = tok // chips

    def kernel(x_ref, *rest):
        outs, sem = rest[:chips], rest[chips]
        _, a, _ = place()
        copies = [
            pltpu.make_async_copy(
                x_ref.at[pl.ds(pl.multiple_of((a ^ u) * part, part), part)], outs[u], sem.at[u]
            )
            for u in range(chips)
        ]
        for copy in copies:
            copy.start()
        for copy in copies:
            copy.wait()

    return call(
        kernel,
        "quarters",
        [((part, width), BF16)] * chips,
        in_hbm(cot),
        specs=[ANY],
        scratch=[pltpu.SemaphoreType.DMA((chips,))],
    )


def choose(pieces, order, after=()):
    n = len(pieces)

    def kernel(*refs):
        r, a, _ = place()
        for i, t in enumerate(order):
            for u in range(n):

                @pl.when((r ^ a ^ t) == u)
                def _():
                    refs[n + i][...] = refs[u][...]

    shape = (pieces[0].shape, BF16)
    return call(kernel, "choose", [shape] * len(order), *map(in_vmem, pieces), after=after)


def back_product(own, other, weight, tok, after=()):
    chips = len(own)
    chunk, width = own[0].shape
    part = tok // chips
    blocks = chunk // part
    dr, ff = weight.shape
    step = 512

    def kernel(*refs):
        w_ref, c_ref, out2, out3 = refs[chips + 2 : chips + 6]
        _, a, h = place()
        for w in range(2):
            lanes = pl.ds(pl.multiple_of((h ^ w) * width, width), width)
            for u in range(chips):
                for t in range(blocks):
                    rows = pl.ds(pl.multiple_of(t * tok + (a ^ u) * part, part), part)
                    if w == 0:
                        c_ref[rows, lanes] = refs[u][t * part : (t + 1) * part, :]
                    else:
                        pair, at = ((0, 0), (1, 0), (1, 1), (0, 1))[u]
                        at = at * chunk + t * part
                        c_ref[rows, lanes] = refs[chips + pair][at : at + part, :]
        for j in range(0, ff, step):
            product = jnp.dot(
                c_ref[2 * tok : 4 * tok, :], w_ref[:, j : j + step], preferred_element_type=F32
            ).astype(BF16)
            out2[:, j : j + step] = product[:tok]
            out3[:, j : j + step] = product[tok:]

    return call(
        kernel,
        "back_product",
        [((blocks * tok, dr), BF16)] + [((tok, ff), BF16)] * 2,
        *map(in_vmem, own),
        *map(in_vmem, other),
        in_vmem(weight),
        after=after,
    )


def back_rest(cot, weight, tok, after=()):
    dr, ff = weight.shape
    step = 512

    def kernel(c_ref, w_ref, out0, out1):
        for j in range(0, ff, step):
            product = jnp.dot(
                c_ref[: 2 * tok, :], w_ref[:, j : j + step], preferred_element_type=F32
            ).astype(BF16)
            out0[:, j : j + step] = product[:tok]
            out1[:, j : j + step] = product[tok:]

    return call(
        kernel,
        "back_rest",
        [((tok, ff), BF16)] * 2,
        in_vmem(cot),
        in_vmem(weight),
        after=after,
    )


def out_product(hidden, pairs, weight, pieces, after=()):
    tok, ff = (*hidden, *map(lambda pair: pair[0], pairs))[0].shape
    half = weight.shape[0] // 2
    n = len(hidden)
    flat = [x for pair in pairs for x in pair]
    rows = (n + len(pairs)) * tok
    size = half // pieces
    step = min(size, 512)

    def kernel(*refs):
        w_ref = refs[n + len(flat)]
        outs = refs[n + len(flat) + 1 :]
        sent, own_ref, blocks = outs[:pieces], outs[pieces], outs[pieces + 1 :]
        _, _, h = place()
        for i in range(len(pairs)):
            blocks[i][...] = refs[n + 2 * i][...] + refs[n + 2 * i + 1][...]
        lhs = jnp.concatenate([ref[...] for ref in (*refs[:n], *blocks)], axis=0)
        for own, first in ((False, (1 - h) * half), (True, h * half)):
            for j in range(0, half, step):
                at = pl.ds(pl.multiple_of(first + j, step), step)
                product = lax.dot_general(
                    lhs, w_ref[at, :], (((1,), (1,)), ((), ())), preferred_element_type=F32
                )
                if own:
                    own_ref[:, j : j + step] = product
                else:
                    sent[j // size][:, j % size : j % size + step] = product.astype(BF16)

    return call(
        kernel,
        "out_product",
        [((rows, size), BF16)] * pieces
        + [((rows, half), F32)]
        + [((tok, ff), BF16)] * len(pairs),
        *map(in_vmem, hidden),
        *map(in_vmem, flat),
        in_vmem(weight),
        after=after,
    )


def add_and_pass(pairs, passed=(), after=()):
    flat = [x for pair in pairs for x in pair]

    def kernel(*refs):
        outs = refs[len(flat) + len(passed) :]
        for i in range(len(pairs)):
            outs[i][...] = (
                refs[2 * i][...].astype(F32) + refs[2 * i + 1][...].astype(F32)
            ).astype(BF16)
        for i in range(len(passed)):
            outs[len(pairs) + i][...] = refs[len(flat) + i][...]

    shapes = [(pair[0].shape, BF16) for pair in pairs] + [(x.shape, BF16) for x in passed]
    return call(
        kernel, "add_and_pass", shapes, *map(in_vmem, flat), *map(in_vmem, passed), after=after
    )


def pair_sum(owns, received, tok, chips, after=()):
    width = owns[0].shape[1]
    blocks = sum(own.shape[0] for own in owns) // tok
    part = tok // chips
    flat = [x for chunk in received for x in chunk]

    def kernel(*refs):
        outs = refs[len(owns) + len(flat) :]
        _, a, _ = place()
        to, at_piece = 0, len(owns)
        for i, chunk in enumerate(received):
            step = chunk[0].shape[1]
            for b in range(owns[i].shape[0] // tok):
                for u in range(chips):
                    at = pl.ds(pl.multiple_of(b * tok + (a ^ u) * part, part), part)
                    for j in range(len(chunk)):
                        lanes = slice(j * step, (j + 1) * step)
                        outs[u][to * part : (to + 1) * part, lanes] = (
                            refs[i][at, lanes] + refs[at_piece + j][at, :].astype(F32)
                        ).astype(BF16)
                to += 1
            at_piece += len(chunk)

    return call(
        kernel,
        "pair_sum",
        [((blocks * part, width), BF16)] * chips,
        *map(in_vmem, owns),
        *map(in_vmem, flat),
        after=after,
    )


def plane_sum(pieces, part, after=()):
    n = len(pieces)
    blocks = pieces[0].shape[0] // part

    def kernel(*refs):
        outs = refs[n:]
        r, a, _ = place()
        for t in range(blocks):
            at = slice(t * part, (t + 1) * part)
            total = refs[0][at, :].astype(F32)
            for ref in refs[1:n]:
                total += ref[at, :].astype(F32)
            total = total.astype(BF16)
            for k in range(blocks):

                @pl.when((r ^ a ^ k) == t)
                def _():
                    outs[k][...] = total

    shape = ((part, pieces[0].shape[1]), BF16)
    return call(kernel, "plane_sum", [shape] * blocks, *map(in_vmem, pieces), after=after)


def assemble(pieces, after=()):
    n = len(pieces)
    part, width = pieces[0].shape

    def kernel(*refs):
        r, _, _ = place()
        for k in range(n):
            refs[-1][pl.ds(pl.multiple_of((r ^ k) * part, part), part), :] = refs[k][...]

    return pl.pallas_call(
        kernel,
        in_specs=[VMEM] * n + [ANY] * len(after),
        out_specs=VMEM,
        out_shape=jax.ShapeDtypeStruct((n * part, width), BF16),
        compiler_params=PARAMS,
        cost_estimate=pl.CostEstimate(flops=COSTS["assemble"], bytes_accessed=0, transcendentals=0),
        name="assemble",
    )(*map(in_vmem, pieces), *after)


def down_gradient(cot, hidden, mask_rows, half, begun=None, after=()):
    n = len(hidden)
    tok, ff = hidden[0].shape
    tokens, dr = cot.shape
    tile_r = mask_rows.shape[0]
    size = dr // tile_r
    step = dr // 4
    extra = ([] if begun is None else [begun]) + list(after)

    def kernel(c_ref, *refs):
        m_ref = refs[n]
        o_ref, t_ref, h_ref = refs[-3:]
        i = pl.program_id(0)
        t_ref[...] = jnp.zeros(t_ref.shape, BF16)

        @pl.when(i == 0)
        def _():
            for t in range(n):
                h_ref[t * tok : (t + 1) * tok, :] = refs[t][...]

        product = lax.dot_general(
            c_ref[...], h_ref[...], (((0,), (0,)), ((), ())), preferred_element_type=F32
        )
        for b in range(step // size):
            kept = m_ref[pl.ds((2 * half + i) * (step // size) + b, 1), :] > 0
            at = slice(b * size, (b + 1) * size)
            o_ref[at, :] = jnp.where(kept, product[at, :], 0.0).astype(BF16)

    return pl.pallas_call(
        kernel,
        grid=(2,),
        in_specs=[pl.BlockSpec((tokens, step), lambda i: (0, 2 * half + i))]
        + [VMEM] * (n + 1)
        + [ANY] * len(extra),
        out_specs=[pl.BlockSpec((step, ff), lambda i: (2 * half + i, 0)), VMEM],
        out_shape=[jax.ShapeDtypeStruct((dr, ff), BF16), pltpu.VMEM((16, 128), BF16)],
        scratch_shapes=[pltpu.VMEM((tokens, ff), BF16)],
        input_output_aliases={} if begun is None else {n + 2: 0},
        compiler_params=PARAMS,
        cost_estimate=pl.CostEstimate(flops=COSTS["down_gradient"], bytes_accessed=0, transcendentals=0),
        name="down_gradient",
    )(in_vmem(cot), *map(in_vmem, hidden), in_vmem(mask_rows), *extra)


def fast_body(gate_pre, up_pre, down_weight, block_mask, cotangent):
    rows, chips = 4, 4
    tok = gate_pre.shape[0]
    part = tok // chips

    def over_row(x, t, senders=range(4)):
        return lax.ppermute(x, "row", [(i, i ^ t) for i in senders])

    def over_chips(x, u):
        return lax.ppermute(x, "col", [(j, j ^ (2 * u)) for j in range(2 * chips)])

    def over_core(x):
        return lax.ppermute(x, "col", [(j, j ^ 1) for j in range(2 * chips)])

    ends, inner = (0, 3), (1, 2)

    mine = quarters(cotangent, chips)
    spread = [mine[0]] + [over_chips(mine[u], u) for u in range(1, chips)]
    first, dg, du, mask_rows = gated(
        gate_pre, up_pre, block_mask, down_weight.shape[1], after=[mine[0]]
    )
    weight = masked_weight(down_weight, mask_rows, 0, after=[first])
    ours = choose(spread, (3, 2, 1, 0), after=[weight])
    cot = {t: over_row(x, t) for t, x in zip((3, 2, 1), ours)}
    cot[0] = ours[3]
    weight = masked_weight(down_weight, mask_rows, 1, weight, after=[ours[0]])

    mine = stack([cot[t] for t in range(rows)], after=[weight])
    same = [mine] + [over_chips(mine, u) for u in range(1, chips)]

    hidden = {0: add_and_pass([], [first], after=[mine])[0]}
    hidden[1] = over_row(hidden[0], 1)
    inner3 = over_row(hidden[0], 3, inner)
    inner2 = over_row(hidden[1], 3, inner)
    ends2 = over_row(inner3, 1, inner)

    other = [over_core(stack([same[0], same[3]])), over_core(stack([same[1], same[2]]))]
    cot, back2, back3 = back_product(same, other, weight, tok, after=[hidden[1], inner3])

    first3 = over_row(back3, 1, ends)
    first2 = over_row(back2, 1, ends)
    *sent, own01 = out_product([hidden[0], hidden[1]], [], weight, 1, after=[back3])
    received = [[over_core(x) for x in sent]]
    back0, back1 = back_rest(cot, weight, tok, after=[own01])
    (inner2,) = add_and_pass([], [inner2], after=[back1])
    ends3 = over_row(inner2, 1, inner)
    (hidden[2],) = add_and_pass([(inner2, ends2)], after=[inner2])
    (to_pass,) = add_and_pass([(back2, first3)], after=[hidden[2]])
    second = over_row(to_pass, 3, inner)
    *sent, own23, hidden[3] = out_product(
        [hidden[2]], [[inner3, ends3]], weight, 2, after=[to_pass]
    )
    received.append([over_core(x) for x in sent])
    (to_inner,) = add_and_pass([(back3, first2)], after=[own23])
    across = over_row(to_inner, 3, inner)
    pieces = pair_sum([own01, own23], received, tok, chips)
    pieces = [pieces[0]] + [over_chips(pieces[u], u) for u in range(1, chips)]
    (to_near,) = add_and_pass([(back1, second)], after=[pieces[0]])
    beside = over_row(to_near, 1)
    tokens = [hidden[t] for t in range(rows)]
    d_down, done = down_gradient(cot, tokens, mask_rows, 0, after=[to_near])
    d_down, done = down_gradient(cot, tokens, mask_rows, 1, d_down, after=[done])
    ready = plane_sum(pieces, part, after=[done])
    d_gate, d_up, last = gradients([back0, beside, across], dg, du, after=[ready[0]])

    width = 2 * chips
    placed = [
        lax.ppermute(
            ready[k],
            ("row", "col"),
            [
                (r * width + 2 * a + h, (a ^ k) * width + 2 * r + h)
                for r in range(rows)
                for a in range(chips)
                for h in range(2)
            ],
        )
        for k in range(rows)
    ]
    output = assemble(placed, after=[last])

    return output, d_gate, d_up, d_down


def rounded_f32(values):
    return lax.optimization_barrier(values.astype(BF16)).astype(F32)


def general_body(gate_pre, up_pre, down_weight, block_mask, cotangent):
    tok_rows, ff_cols = gate_pre.shape
    d_rows = down_weight.shape[0]
    block_size = d_rows // block_mask.shape[0]
    gate_wide = gate_pre.astype(F32)
    up_wide = up_pre.astype(F32)
    activated = jax.nn.silu(gate_wide)
    hidden = (activated * up_wide).astype(BF16)
    expand = jnp.repeat(jnp.repeat(block_mask, block_size, axis=0), block_size, axis=1)
    masked = jnp.where(expand > 0, down_weight, jnp.zeros_like(down_weight))
    cot_row = lax.all_gather(cotangent, "col", axis=1, tiled=True)
    cot_all = lax.all_to_all(cot_row, "row", split_axis=1, concat_axis=0, tiled=True)
    panel = lax.all_gather(masked, "row", axis=0, tiled=True)
    y_partial = lax.dot_general(
        hidden, panel, (((1,), (1,)), ((), ())), preferred_element_type=F32
    )
    shards = panel.shape[0] // d_rows
    per_shard = jnp.einsum(
        "tnd,ndf->ntf",
        cot_row.reshape(tok_rows, shards, d_rows),
        panel.reshape(shards, d_rows, ff_cols),
        preferred_element_type=F32,
    )
    d_hidden = jnp.sum(rounded_f32(per_shard), axis=0)
    hidden_all = lax.all_gather(hidden, "row", axis=0, tiled=True)
    grad_full = lax.dot_general(
        cot_all, hidden_all, (((0,), (0,)), ((), ())), preferred_element_type=F32
    )
    output = lax.psum_scatter(y_partial.astype(BF16), "col", scatter_dimension=1, tiled=True)
    sigmoid_g = jax.nn.sigmoid(gate_wide)
    d_gate = (d_hidden * up_wide * sigmoid_g * (1.0 + gate_wide * (1.0 - sigmoid_g))).astype(BF16)
    d_up = (d_hidden * activated).astype(BF16)
    d_down = jnp.where(expand > 0, grad_full, jnp.zeros_like(grad_full)).astype(BF16)
    return output, d_gate, d_up, d_down


def solution(mesh):
    spec = P("row", "col")
    small = mesh.shape["row"] == 4 and mesh.shape["col"] == 8
    return jax.shard_map(
        fast_body if small else general_body,
        mesh=mesh,
        in_specs=(spec,) * 5,
        out_specs=(spec,) * 4,
        check_vma=False,
    )
```

```python
import jax
import jax.numpy as jnp
from jax import lax
from jax.experimental import pallas as pl
from jax.experimental.pallas import tpu as pltpu
from jax.sharding import PartitionSpec as P

F32 = jnp.float32
BF16 = jnp.bfloat16
VMEM = pl.BlockSpec(memory_space=pltpu.VMEM)
SMEM = pl.BlockSpec(memory_space=pltpu.SMEM)
PARAMS = pltpu.CompilerParams(vmem_limit_bytes=16 * 2**20)


ANY = pl.BlockSpec(memory_space=pl.ANY)


def in_vmem(array):
    return pltpu.with_memory_space_constraint(array, pltpu.VMEM)


def in_hbm(array):
    return pltpu.with_memory_space_constraint(array, pltpu.HBM)


def place():
    col = lax.axis_index("col")
    return lax.axis_index("row"), col // 2, col % 2


COSTS = {'quarters': 311445000, 'gated': 588285000, 'masked_weight': 761310000, 'choose': 34605000, 'stack': 34605000, 'back_product': 865125000, 'back_rest': 830520000, 'out_product': 830520000, 'pair_sum': 69210000, 'plane_sum': 3460500000, 'add_and_pass': 69210000, 'down_gradient': 1418804999, 'gradients': 588285000, 'assemble': 242235000, 'to_vmem': 311445000}


def call(kernel, name, outs, *args, specs=None, scratch=(), flops=0, moved=0, after=()):
    n, m = len(args), len(args) + len(after)

    def body(*refs):
        kernel(*refs[:n], *refs[m:])

    return pl.pallas_call(
        body,
        in_specs=(specs or [VMEM] * n) + [pl.BlockSpec(memory_space=pl.ANY)] * len(after),
        out_specs=[VMEM] * len(outs),
        out_shape=[pltpu.VMEM(shape, dtype) for shape, dtype in outs],
        scratch_shapes=list(scratch),
        compiler_params=PARAMS,
        cost_estimate=pl.CostEstimate(flops=COSTS[name], bytes_accessed=0, transcendentals=0),
        name=name,
    )(*args, *after)


def masked_weight(weight, mask_rows, half, begun=None, after=()):
    rows, cols = weight.shape
    tile_r = mask_rows.shape[0]
    size = rows // tile_r
    mine = range(half * tile_r // 2, (half + 1) * tile_r // 2)
    extra = [] if begun is None else [in_vmem(begun)]

    def kernel(w_ref, m_ref, *refs):
        o_ref, sem = refs[-2:]

        def copy(i):
            at = pl.ds(i * size, size)
            return pltpu.make_async_copy(w_ref.at[at], o_ref.at[at], sem.at[i - mine[0]])

        for i in mine:
            copy(i).start()
        for i in mine:
            copy(i).wait()
            at = slice(i * size, (i + 1) * size)
            o_ref[at, :] = jnp.where(m_ref[i : i + 1, :] > 0, o_ref[at, :], jnp.zeros((), BF16))

    return pl.pallas_call(
        kernel,
        in_specs=[ANY, VMEM] + [VMEM] * len(extra) + [ANY] * len(after),
        out_specs=VMEM,
        out_shape=pltpu.VMEM((rows, cols), BF16),
        input_output_aliases={} if begun is None else {2: 0},
        scratch_shapes=[pltpu.SemaphoreType.DMA((len(mine),))],
        compiler_params=PARAMS,
        cost_estimate=pl.CostEstimate(flops=COSTS["masked_weight"], bytes_accessed=0, transcendentals=0),
        name="masked_weight",
    )(in_hbm(weight), in_vmem(mask_rows), *extra, *after)


def gated(gate, up, mask, width, after=()):
    tile_r, tile_c = mask.shape
    size = width // tile_c

    def kernel(g_hbm, u_hbm, m_hbm, o_ref, dg_ref, du_ref, rows_ref, g_ref, u_ref, m_ref, sem):
        copies = [
            pltpu.make_async_copy(m_hbm, m_ref, sem.at[2]),
            pltpu.make_async_copy(g_hbm, g_ref, sem.at[0]),
            pltpu.make_async_copy(u_hbm, u_ref, sem.at[1]),
        ]
        for copy in copies:
            copy.start()
        copies[0].wait()
        for i in range(tile_r):
            for j in range(tile_c):
                rows_ref[i : i + 1, j * size : (j + 1) * size] = jnp.full(
                    (1, size), m_ref[i, j], jnp.int32
                )
        for copy in copies[1:]:
            copy.wait()
        g = g_ref[...].astype(F32)
        u = u_ref[...].astype(F32)
        s = 1.0 / (1.0 + jnp.exp(-g))
        o_ref[...] = (g * s * u).astype(BF16)
        dg_ref[...] = u * s * (1.0 + g * (1.0 - s))
        du_ref[...] = g * s

    return call(
        kernel,
        "gated",
        [
            (gate.shape, BF16),
            (gate.shape, F32),
            (gate.shape, F32),
            ((tile_r, width), jnp.int32),
        ],
        in_hbm(gate),
        in_hbm(up),
        in_hbm(mask),
        specs=[ANY] * 3,
        scratch=[pltpu.VMEM(gate.shape, BF16)] * 2
        + [pltpu.SMEM(mask.shape, jnp.int32), pltpu.SemaphoreType.DMA((3,))],
        after=after,
    )


def gradients(shares, dg, du, after=()):
    rows, cols = dg.shape
    n = len(shares)
    step = rows // 4

    def kernel(*refs):
        dg_ref, du_ref = refs[n : n + 2]
        out_g, out_u, token = refs[-3:]
        token[...] = jnp.zeros(token.shape, BF16)
        total = refs[0][...].astype(F32)
        for ref in refs[1:n]:
            total += ref[...].astype(F32)
        out_g[...] = (total * dg_ref[...]).astype(BF16)
        out_u[...] = (total * du_ref[...]).astype(BF16)

    block = pl.BlockSpec((step, cols), lambda i: (i, 0))
    return pl.pallas_call(
        kernel,
        grid=(rows // step,),
        in_specs=[block] * (n + 2) + [ANY] * len(after),
        out_specs=[block] * 2 + [VMEM],
        out_shape=[jax.ShapeDtypeStruct((rows, cols), BF16)] * 2
        + [pltpu.VMEM((16, 128), BF16)],
        compiler_params=PARAMS,
        cost_estimate=pl.CostEstimate(flops=COSTS["gradients"], bytes_accessed=0, transcendentals=0),
        name="gradients",
    )(*map(in_vmem, shares), in_vmem(dg), in_vmem(du), *after)


def stack(pieces, after=()):
    part, width = pieces[0].shape

    def kernel(*refs):
        for i in range(len(pieces)):
            refs[-1][i * part : (i + 1) * part, :] = refs[i][...]

    shape = (len(pieces) * part, width)
    return call(kernel, "stack", [(shape, BF16)], *map(in_vmem, pieces), after=after)[0]


def quarters(cot, chips):
    tok, width = cot.shape
    part = tok // chips

    def kernel(x_ref, *rest):
        outs, sem = rest[:chips], rest[chips]
        _, a, _ = place()
        copies = [
            pltpu.make_async_copy(
                x_ref.at[pl.ds(pl.multiple_of((a ^ u) * part, part), part)], outs[u], sem.at[u]
            )
            for u in range(chips)
        ]
        for copy in copies:
            copy.start()
        for copy in copies:
            copy.wait()

    return call(
        kernel,
        "quarters",
        [((part, width), BF16)] * chips,
        in_hbm(cot),
        specs=[ANY],
        scratch=[pltpu.SemaphoreType.DMA((chips,))],
    )


def choose(pieces, order, after=()):
    n = len(pieces)

    def kernel(*refs):
        r, a, _ = place()
        for i, t in enumerate(order):
            for u in range(n):

                @pl.when((r ^ a ^ t) == u)
                def _():
                    refs[n + i][...] = refs[u][...]

    shape = (pieces[0].shape, BF16)
    return call(kernel, "choose", [shape] * len(order), *map(in_vmem, pieces), after=after)


def back_product(own, other, weight, tok, after=()):
    chips = len(own)
    chunk, width = own[0].shape
    part = tok // chips
    blocks = chunk // part
    dr, ff = weight.shape
    step = 512

    def kernel(*refs):
        w_ref, c_ref, out2, out3 = refs[chips + 2 : chips + 6]
        _, a, h = place()
        for w in range(2):
            lanes = pl.ds(pl.multiple_of((h ^ w) * width, width), width)
            for u in range(chips):
                for t in range(blocks):
                    rows = pl.ds(pl.multiple_of(t * tok + (a ^ u) * part, part), part)
                    if w == 0:
                        c_ref[rows, lanes] = refs[u][t * part : (t + 1) * part, :]
                    else:
                        pair, at = ((0, 0), (1, 0), (1, 1), (0, 1))[u]
                        at = at * chunk + t * part
                        c_ref[rows, lanes] = refs[chips + pair][at : at + part, :]
        for j in range(0, ff, step):
            product = jnp.dot(
                c_ref[2 * tok : 4 * tok, :], w_ref[:, j : j + step], preferred_element_type=F32
            ).astype(BF16)
            out2[:, j : j + step] = product[:tok]
            out3[:, j : j + step] = product[tok:]

    return call(
        kernel,
        "back_product",
        [((blocks * tok, dr), BF16)] + [((tok, ff), BF16)] * 2,
        *map(in_vmem, own),
        *map(in_vmem, other),
        in_vmem(weight),
        after=after,
    )


def back_rest(cot, weight, tok, after=()):
    dr, ff = weight.shape
    step = 512

    def kernel(c_ref, w_ref, out0, out1):
        for j in range(0, ff, step):
            product = jnp.dot(
                c_ref[: 2 * tok, :], w_ref[:, j : j + step], preferred_element_type=F32
            ).astype(BF16)
            out0[:, j : j + step] = product[:tok]
            out1[:, j : j + step] = product[tok:]

    return call(
        kernel,
        "back_rest",
        [((tok, ff), BF16)] * 2,
        in_vmem(cot),
        in_vmem(weight),
        after=after,
    )


def out_product(hidden, pairs, weight, pieces, after=()):
    tok, ff = (*hidden, *map(lambda pair: pair[0], pairs))[0].shape
    half = weight.shape[0] // 2
    n = len(hidden)
    flat = [x for pair in pairs for x in pair]
    rows = (n + len(pairs)) * tok
    size = half // pieces
    step = min(size, 512)

    def kernel(*refs):
        w_ref = refs[n + len(flat)]
        outs = refs[n + len(flat) + 1 :]
        sent, own_ref, blocks = outs[:pieces], outs[pieces], outs[pieces + 1 :]
        _, _, h = place()
        for i in range(len(pairs)):
            blocks[i][...] = refs[n + 2 * i][...] + refs[n + 2 * i + 1][...]
        lhs = jnp.concatenate([ref[...] for ref in (*refs[:n], *blocks)], axis=0)
        for own, first in ((False, (1 - h) * half), (True, h * half)):
            for j in range(0, half, step):
                at = pl.ds(pl.multiple_of(first + j, step), step)
                product = lax.dot_general(
                    lhs, w_ref[at, :], (((1,), (1,)), ((), ())), preferred_element_type=F32
                )
                if own:
                    own_ref[:, j : j + step] = product
                else:
                    sent[j // size][:, j % size : j % size + step] = product.astype(BF16)

    return call(
        kernel,
        "out_product",
        [((rows, size), BF16)] * pieces
        + [((rows, half), F32)]
        + [((tok, ff), BF16)] * len(pairs),
        *map(in_vmem, hidden),
        *map(in_vmem, flat),
        in_vmem(weight),
        after=after,
    )


def add_and_pass(pairs, passed=(), after=()):
    flat = [x for pair in pairs for x in pair]

    def kernel(*refs):
        outs = refs[len(flat) + len(passed) :]
        for i in range(len(pairs)):
            outs[i][...] = (
                refs[2 * i][...].astype(F32) + refs[2 * i + 1][...].astype(F32)
            ).astype(BF16)
        for i in range(len(passed)):
            outs[len(pairs) + i][...] = refs[len(flat) + i][...]

    shapes = [(pair[0].shape, BF16) for pair in pairs] + [(x.shape, BF16) for x in passed]
    return call(
        kernel, "add_and_pass", shapes, *map(in_vmem, flat), *map(in_vmem, passed), after=after
    )


def pair_sum(owns, received, tok, chips, after=()):
    width = owns[0].shape[1]
    blocks = sum(own.shape[0] for own in owns) // tok
    part = tok // chips
    flat = [x for chunk in received for x in chunk]

    def kernel(*refs):
        outs = refs[len(owns) + len(flat) :]
        _, a, _ = place()
        to, at_piece = 0, len(owns)
        for i, chunk in enumerate(received):
            step = chunk[0].shape[1]
            for b in range(owns[i].shape[0] // tok):
                for u in range(chips):
                    at = pl.ds(pl.multiple_of(b * tok + (a ^ u) * part, part), part)
                    for j in range(len(chunk)):
                        lanes = slice(j * step, (j + 1) * step)
                        outs[u][to * part : (to + 1) * part, lanes] = (
                            refs[i][at, lanes] + refs[at_piece + j][at, :].astype(F32)
                        ).astype(BF16)
                to += 1
            at_piece += len(chunk)

    return call(
        kernel,
        "pair_sum",
        [((blocks * part, width), BF16)] * chips,
        *map(in_vmem, owns),
        *map(in_vmem, flat),
        after=after,
    )


def plane_sum(pieces, part, after=()):
    n = len(pieces)
    blocks = pieces[0].shape[0] // part

    def kernel(*refs):
        outs = refs[n:]
        r, a, _ = place()
        for t in range(blocks):
            at = slice(t * part, (t + 1) * part)
            total = refs[0][at, :].astype(F32)
            for ref in refs[1:n]:
                total += ref[at, :].astype(F32)
            total = total.astype(BF16)
            for k in range(blocks):

                @pl.when((r ^ a ^ k) == t)
                def _():
                    outs[k][...] = total

    shape = ((part, pieces[0].shape[1]), BF16)
    return call(kernel, "plane_sum", [shape] * blocks, *map(in_vmem, pieces), after=after)


def assemble(pieces, after=()):
    n = len(pieces)
    part, width = pieces[0].shape

    def kernel(*refs):
        r, _, _ = place()
        for k in range(n):
            refs[-1][pl.ds(pl.multiple_of((r ^ k) * part, part), part), :] = refs[k][...]

    return pl.pallas_call(
        kernel,
        in_specs=[VMEM] * n + [ANY] * len(after),
        out_specs=VMEM,
        out_shape=jax.ShapeDtypeStruct((n * part, width), BF16),
        compiler_params=PARAMS,
        cost_estimate=pl.CostEstimate(flops=COSTS["assemble"], bytes_accessed=0, transcendentals=0),
        name="assemble",
    )(*map(in_vmem, pieces), *after)


def down_gradient(cot, hidden, mask_rows, half, begun=None, after=()):
    n = len(hidden)
    tok, ff = hidden[0].shape
    tokens, dr = cot.shape
    tile_r = mask_rows.shape[0]
    size = dr // tile_r
    step = dr // 4
    extra = ([] if begun is None else [begun]) + list(after)

    def kernel(c_ref, *refs):
        m_ref = refs[n]
        o_ref, t_ref, h_ref = refs[-3:]
        i = pl.program_id(0)
        t_ref[...] = jnp.zeros(t_ref.shape, BF16)

        @pl.when(i == 0)
        def _():
            for t in range(n):
                h_ref[t * tok : (t + 1) * tok, :] = refs[t][...]

        product = lax.dot_general(
            c_ref[...], h_ref[...], (((0,), (0,)), ((), ())), preferred_element_type=F32
        )
        for b in range(step // size):
            kept = m_ref[pl.ds((2 * half + i) * (step // size) + b, 1), :] > 0
            at = slice(b * size, (b + 1) * size)
            o_ref[at, :] = jnp.where(kept, product[at, :], 0.0).astype(BF16)

    return pl.pallas_call(
        kernel,
        grid=(2,),
        in_specs=[pl.BlockSpec((tokens, step), lambda i: (0, 2 * half + i))]
        + [VMEM] * (n + 1)
        + [ANY] * len(extra),
        out_specs=[pl.BlockSpec((step, ff), lambda i: (2 * half + i, 0)), VMEM],
        out_shape=[jax.ShapeDtypeStruct((dr, ff), BF16), pltpu.VMEM((16, 128), BF16)],
        scratch_shapes=[pltpu.VMEM((tokens, ff), BF16)],
        input_output_aliases={} if begun is None else {n + 2: 0},
        compiler_params=PARAMS,
        cost_estimate=pl.CostEstimate(flops=COSTS["down_gradient"], bytes_accessed=0, transcendentals=0),
        name="down_gradient",
    )(in_vmem(cot), *map(in_vmem, hidden), in_vmem(mask_rows), *extra)


def fast_body(gate_pre, up_pre, down_weight, block_mask, cotangent):
    rows, chips = 4, 4
    tok = gate_pre.shape[0]
    part = tok // chips

    def over_row(x, t, senders=range(4)):
        return lax.ppermute(x, "row", [(i, i ^ t) for i in senders])

    def over_chips(x, u):
        return lax.ppermute(x, "col", [(j, j ^ (2 * u)) for j in range(2 * chips)])

    def over_core(x):
        return lax.ppermute(x, "col", [(j, j ^ 1) for j in range(2 * chips)])

    ends, inner = (0, 3), (1, 2)

    mine = quarters(cotangent, chips)
    spread = [mine[0]] + [over_chips(mine[u], u) for u in range(1, chips)]
    first, dg, du, mask_rows = gated(
        gate_pre, up_pre, block_mask, down_weight.shape[1], after=[mine[0]]
    )
    weight = masked_weight(down_weight, mask_rows, 0, after=[first])
    ours = choose(spread, (3, 2, 1, 0), after=[weight])
    cot = {t: over_row(x, t) for t, x in zip((3, 2, 1), ours)}
    cot[0] = ours[3]
    weight = masked_weight(down_weight, mask_rows, 1, weight, after=[ours[0]])

    mine = stack([cot[t] for t in range(rows)], after=[weight])
    same = [mine] + [over_chips(mine, u) for u in range(1, chips)]

    hidden = {0: add_and_pass([], [first], after=[mine])[0]}
    hidden[1] = over_row(hidden[0], 1)
    inner3 = over_row(hidden[0], 3, inner)
    inner2 = over_row(hidden[1], 3, inner)
    ends2 = over_row(inner3, 1, inner)

    other = [over_core(stack([same[0], same[3]])), over_core(stack([same[1], same[2]]))]
    cot, back2, back3 = back_product(same, other, weight, tok, after=[hidden[1], inner3])

    first3 = over_row(back3, 1, ends)
    first2 = over_row(back2, 1, ends)
    *sent, own01 = out_product([hidden[0], hidden[1]], [], weight, 1, after=[back3])
    received = [[over_core(x) for x in sent]]
    back0, back1 = back_rest(cot, weight, tok, after=[own01])
    (inner2,) = add_and_pass([], [inner2], after=[back1])
    ends3 = over_row(inner2, 1, inner)
    (hidden[2],) = add_and_pass([(inner2, ends2)], after=[inner2])
    (to_pass,) = add_and_pass([(back2, first3)], after=[hidden[2]])
    second = over_row(to_pass, 3, inner)
    *sent, own23, hidden[3] = out_product(
        [hidden[2]], [[inner3, ends3]], weight, 2, after=[to_pass]
    )
    received.append([over_core(x) for x in sent])
    (to_inner,) = add_and_pass([(back3, first2)], after=[own23])
    across = over_row(to_inner, 3, inner)
    pieces = pair_sum([own01, own23], received, tok, chips, after=[to_inner])
    pieces = [pieces[0]] + [over_chips(pieces[u], u) for u in range(1, chips)]
    (to_near,) = add_and_pass([(back1, second)], after=[pieces[0]])
    beside = over_row(to_near, 1)
    tokens = [hidden[t] for t in range(rows)]
    d_down, done = down_gradient(cot, tokens, mask_rows, 0, after=[to_near])
    d_down, done = down_gradient(cot, tokens, mask_rows, 1, d_down, after=[done])
    ready = plane_sum(pieces, part, after=[done])
    d_gate, d_up, last = gradients([back0, beside, across], dg, du, after=[ready[0]])

    width = 2 * chips
    placed = [
        lax.ppermute(
            ready[k],
            ("row", "col"),
            [
                (r * width + 2 * a + h, (a ^ k) * width + 2 * r + h)
                for r in range(rows)
                for a in range(chips)
                for h in range(2)
            ],
        )
        for k in range(rows)
    ]
    output = assemble(placed, after=[last])

    return output, d_gate, d_up, d_down


def rounded_f32(values):
    return lax.optimization_barrier(values.astype(BF16)).astype(F32)


def general_body(gate_pre, up_pre, down_weight, block_mask, cotangent):
    tok_rows, ff_cols = gate_pre.shape
    d_rows = down_weight.shape[0]
    block_size = d_rows // block_mask.shape[0]
    gate_wide = gate_pre.astype(F32)
    up_wide = up_pre.astype(F32)
    activated = jax.nn.silu(gate_wide)
    hidden = (activated * up_wide).astype(BF16)
    expand = jnp.repeat(jnp.repeat(block_mask, block_size, axis=0), block_size, axis=1)
    masked = jnp.where(expand > 0, down_weight, jnp.zeros_like(down_weight))
    cot_row = lax.all_gather(cotangent, "col", axis=1, tiled=True)
    cot_all = lax.all_to_all(cot_row, "row", split_axis=1, concat_axis=0, tiled=True)
    panel = lax.all_gather(masked, "row", axis=0, tiled=True)
    y_partial = lax.dot_general(
        hidden, panel, (((1,), (1,)), ((), ())), preferred_element_type=F32
    )
    shards = panel.shape[0] // d_rows
    per_shard = jnp.einsum(
        "tnd,ndf->ntf",
        cot_row.reshape(tok_rows, shards, d_rows),
        panel.reshape(shards, d_rows, ff_cols),
        preferred_element_type=F32,
    )
    d_hidden = jnp.sum(rounded_f32(per_shard), axis=0)
    hidden_all = lax.all_gather(hidden, "row", axis=0, tiled=True)
    grad_full = lax.dot_general(
        cot_all, hidden_all, (((0,), (0,)), ((), ())), preferred_element_type=F32
    )
    output = lax.psum_scatter(y_partial.astype(BF16), "col", scatter_dimension=1, tiled=True)
    sigmoid_g = jax.nn.sigmoid(gate_wide)
    d_gate = (d_hidden * up_wide * sigmoid_g * (1.0 + gate_wide * (1.0 - sigmoid_g))).astype(BF16)
    d_up = (d_hidden * activated).astype(BF16)
    d_down = jnp.where(expand > 0, grad_full, jnp.zeros_like(grad_full)).astype(BF16)
    return output, d_gate, d_up, d_down


def solution(mesh):
    spec = P("row", "col")
    small = mesh.shape["row"] == 4 and mesh.shape["col"] == 8
    return jax.shard_map(
        fast_body if small else general_body,
        mesh=mesh,
        in_specs=(spec,) * 5,
        out_specs=(spec,) * 4,
        check_vma=False,
    )
```
